256 devices in a mesh: ctx: 32 (over z, x_hi, core), tp: 8 (over x_lo, y).
Axes of the slice: x: 4 (x_hi: 2, x_lo: 2; x = x_hi * 2 + x_lo), y: 4, z: 8, core: 2. Of those that a mesh axis runs over, the one named last changes fastest.
Arguments:
- features: bfloat16 [3, 8192, 8192], P(None, 'ctx', 'tp'), may hold values from -6 to 6
- short_filter: bfloat16 [3, 3, 8192], P(None, None, 'tp'), may hold values from -3.5 to 3.5
- long_filter: bfloat16 [512, 128], P('tp'), may hold values from -0.5 to 0.5
- out_weight: bfloat16 [8192, 4096], P('tp'), may hold values from -0.0625 to 0.0625
- out_cotangent: bfloat16 [8192, 4096], P('ctx', 'tp'), may hold values from -6 to 6
Outputs:
- mixed: bfloat16 [8192, 4096], P('ctx', 'tp')
- feature_grads: bfloat16 [3, 8192, 8192], P(None, 'ctx', 'tp')
- filter_grad: float32 [512, 128], P('tp')
The draws below stay inside these ranges and needn't reach their ends.
All inputs are finite; a program needn't handle non-finite values.
Results may differ from the reference program's by a relative error of at most 0.02.
Values may be sent and summed in bfloat16 or wider, within the bound.
A program may use at most 128 MiB of HBM per device.

```python
import jax
import jax.numpy as jnp
from jax import lax

CH = 8192
OUTW = 4096
GROUP = 16
FILT = 128
SHORT = 3
TOKENS = 8192
GROUPS = 512
N_TP = 8


def shard_levels(key, shape, pieces, low, largest):
    def one(position, parts):
        heights = jax.random.uniform(jax.random.fold_in(jax.random.fold_in(key, 6), position), (parts,), jnp.float32, low / len(pieces), largest / len(pieces))
        return jnp.repeat(jnp.exp(heights), shape[position] // parts).reshape((-1,) + (1,) * (len(shape) - position - 1))

    factor_of = one(*pieces[0])
    for cut in pieces[1:]:
        factor_of = factor_of * one(*cut)
    return factor_of


def normal_values(stream_key, dims, width, limit, split=(), kind=jnp.bfloat16):
    result = jax.random.normal(stream_key, dims, jnp.float32) * width
    if len(split) > 0:
        result = shard_levels(stream_key, dims, split, -0.22, 0.18) * result
    return jnp.clip(result, min=-limit, max=limit).astype(kind)


def setup_inputs(seed: int = 0) -> dict:
    key_of = jax.random.split(jax.random.key(seed), 6)
    return {
        "features": normal_values(key_of[0], (3, TOKENS, CH), 1.0, 6.0, ((1, 32), (2, 8))),
        "short_filter": normal_values(key_of[1], (3, SHORT, CH), SHORT ** -0.5, 3.5, ((2, 8),)),
        "long_filter": normal_values(key_of[2], (GROUPS, FILT), FILT ** -0.5, 0.5, ((0, 8),)),
        "out_weight": normal_values(key_of[3], (CH, OUTW), CH ** -0.5, 0.0625, ((0, 8),)),
        "out_cotangent": normal_values(key_of[4], (TOKENS, OUTW), 1.0, 6.0, ((0, 32), (1, 8))),
    }


def short_causal(values, short_filter):
    short_taps = short_filter.shape[1]
    padded = jnp.pad(values.astype(jnp.float32), ((0, 0), (short_taps - 1, 0), (0, 0)))
    accumulated = jnp.zeros(values.shape, jnp.float32)
    for lag_index in range(short_taps):
        begin = short_taps - 1 - lag_index
        accumulated = accumulated + short_filter[:, lag_index, None, :].astype(jnp.float32) * padded[:, begin:begin + TOKENS, :]
    return accumulated


def short_anticausal(values, short_filter):
    short_taps = short_filter.shape[1]
    padded = jnp.pad(values.astype(jnp.float32), ((0, 0), (0, short_taps - 1), (0, 0)))
    accumulated = jnp.zeros(values.shape, jnp.float32)
    for lag_index in range(short_taps):
        accumulated = accumulated + short_filter[:, lag_index, None, :].astype(jnp.float32) * padded[:, lag_index:lag_index + TOKENS, :]
    return accumulated


def long_causal(values, channel_taps):
    padded = jnp.pad(values, ((FILT - 1, 0), (0, 0)))

    def add_lag(lag_index, accumulated):
        begin = (FILT - 1 - lag_index).astype(jnp.int32)
        shifted = lax.dynamic_slice_in_dim(padded, begin, TOKENS, 0)
        coefficient = lax.dynamic_index_in_dim(channel_taps, lag_index, 1, keepdims=False)
        return accumulated + coefficient * shifted

    return lax.fori_loop(jnp.int32(0), jnp.int32(FILT), add_lag, jnp.zeros((TOKENS, CH), jnp.float32))


def long_anticausal(values, channel_taps):
    padded = jnp.pad(values, ((0, FILT - 1), (0, 0)))

    def add_lag(lag_index, accumulated):
        begin = lag_index.astype(jnp.int32)
        shifted = lax.dynamic_slice_in_dim(padded, begin, TOKENS, 0)
        coefficient = lax.dynamic_index_in_dim(channel_taps, lag_index, 1, keepdims=False)
        return accumulated + coefficient * shifted

    return lax.fori_loop(jnp.int32(0), jnp.int32(FILT), add_lag, jnp.zeros((TOKENS, CH), jnp.float32))


def reference(features, short_filter, long_filter, out_weight, out_cotangent):
    post = short_causal(features, short_filter).astype(jnp.bfloat16)
    post_float = post.astype(jnp.float32)
    gated = (post_float[1] * post_float[2]).astype(jnp.bfloat16)
    gated_float = gated.astype(jnp.float32)
    channel_taps = jnp.repeat(long_filter.astype(jnp.float32), GROUP, axis=0)
    long_out = long_causal(gated_float, channel_taps)
    mixer = (post_float[0] * long_out).astype(jnp.bfloat16)
    block_width = CH // N_TP
    accumulated = jnp.zeros((TOKENS, OUTW), jnp.float32)
    for part_index in range(N_TP):
        low = part_index * block_width
        partial_sum = jnp.dot(mixer[:, low:low + block_width], out_weight[low:low + block_width], preferred_element_type=jnp.float32)
        rounded = lax.optimization_barrier(partial_sum.astype(jnp.bfloat16))
        accumulated = accumulated + rounded.astype(jnp.float32)
    mixed = accumulated.astype(jnp.bfloat16)
    d_mixer = jnp.dot(out_cotangent, out_weight.T, preferred_element_type=jnp.float32).astype(jnp.bfloat16)
    d_mixer_float = d_mixer.astype(jnp.float32)
    d_query = d_mixer_float * long_out
    d_long = (d_mixer_float * post_float[0]).astype(jnp.bfloat16).astype(jnp.float32)
    d_gated = long_anticausal(d_long, channel_taps)
    gated_padded = jnp.pad(gated_float, ((FILT - 1, 0), (0, 0)))

    def lag_product(lag_index):
        begin = (FILT - 1 - lag_index).astype(jnp.int32)
        shifted = lax.dynamic_slice_in_dim(gated_padded, begin, TOKENS, 0)
        return jnp.sum((d_long * shifted).reshape(TOKENS, GROUPS, GROUP), axis=(0, 2))

    filter_grad = lax.map(lag_product, jnp.arange(FILT, dtype=jnp.int32)).T * (TOKENS * GROUP) ** -0.5
    d_post = jnp.stack([d_query, d_gated * post_float[2], d_gated * post_float[1]])
    feature_grads = short_anticausal(d_post, short_filter).astype(jnp.bfloat16)
    return mixed, feature_grads, filter_grad
```

```python
import functools

import jax
import jax.numpy as jnp
from jax import lax
from jax.experimental import pallas as pl
from jax.experimental.pallas import tpu as pltpu
from jax.sharding import PartitionSpec as P

MESH = pl.DeviceIdType.MESH
F32 = jnp.float32
BF16 = jnp.bfloat16
ROWS = 256
HALF = 128
CHAN = 1024
OUT = 512
N_TP = 8
N_CTX = 32
GROUPS = 64
QR = 48
PR = HALF - QR
TILES = CHAN // 128
PER = 8
CHIPS = N_CTX // 2


def dot(a, b, dims=((1,), (0,))):
    return lax.dot_general(a, b, (dims, ((), ())), preferred_element_type=F32)


def kernel(
    feat,
    sf,
    lf,
    w_hbm,
    cot,
    mixed,
    fgrads,
    filt,
    feats,
    post,
    gated,
    long_out,
    mixer,
    toep,
    vec_a,
    vec_b,
    gath,
    w,
    psum_p,
    psum_q,
    in_up,
    in_own_dn,
    in_own_up,
    in_x,
    in_q,
    in_q_up,
    in_q_own_dn,
    in_q_own_up,
    d_long,
    d_post,
    corr,
    fpart,
    fcore,
    fsum,
    fall,
    fout,
    out_mixed,
    out_grads,
    lsem,
    ag_s,
    ag_r,
    rs_s,
    rs_r,
    halo_s,
    halo_r,
    fg_s,
    fg_r,
):
    ctx = lax.axis_index("ctx")
    me = lax.axis_index("tp")
    core = lax.rem(ctx, 2)
    chip = ctx // 2
    xl = me // 4
    yl = lax.rem(me, 4)
    step = 1 + 2 * core
    back = 3 - 2 * core
    y_up = lax.rem(yl + step, 4)
    y_dn = lax.rem(yl + back, 4)
    y_op = lax.rem(yl + 2, 4)
    own_base = xl * 4
    x_base = 4 - xl * 4
    up = own_base + y_up
    dn = own_base + y_dn
    op = own_base + y_op
    xo = x_base + yl
    xup = x_base + y_up
    xdn = x_base + y_dn
    xop = x_base + y_op
    nxt = lax.rem(ctx + 1, N_CTX)
    prv = lax.rem(ctx + N_CTX - 1, N_CTX)

    load_f = pltpu.make_async_copy(feat, feats.at[:, pl.ds(16, ROWS), :], lsem.at[0])
    load_w = pltpu.make_async_copy(w_hbm, w, lsem.at[1])
    load_c = pltpu.make_async_copy(cot, gath.at[me], lsem.at[2])
    load_f.start()
    load_w.start()
    load_c.start()

    barrier = pltpu.get_barrier_semaphore()
    peers = [(ctx, xo), (ctx, up), (ctx, dn), (nxt, me), (prv, me)]
    for i in range(1, CHIPS):
        peers.append((2 * lax.rem(chip + i, CHIPS) + core, me))
    for peer in peers:
        pl.semaphore_signal(barrier, inc=1, device_id=peer, device_id_type=MESH)

    rows_i = lax.broadcasted_iota(jnp.int32, (HALF, 2 * HALF), 0)
    cols_i = lax.broadcasted_iota(jnp.int32, (HALF, 2 * HALF), 1)
    flip = (cols_i == HALF - rows_i).astype(BF16)
    keep = (cols_i == rows_i).astype(BF16)
    vec_a[...] = dot(lf[...], flip)
    vec_b[...] = dot(lf[...], keep)
    pl.semaphore_wait(barrier, len(peers))

    started = []

    def remote(src, dst, send, recv, dev):
        return pltpu.make_async_remote_copy(
            src_ref=src,
            dst_ref=dst,
            send_sem=send,
            recv_sem=recv,
            device_id=dev,
            device_id_type=MESH,
        )

    QS = (0, QR)
    PS = (QR, PR)

    def ag_view(slot, half, part):
        return gath.at[slot, pl.ds(half * HALF + part[0], part[1]), :]

    def ag_send(n, half, slot, part, dev, src=None):
        there = ag_view(slot, half, part)
        copy = remote(
            there if src is None else src,
            there,
            ag_s.at[half, n],
            ag_r.at[half, n],
            (ctx, dev),
        )
        copy.start()
        started.append(copy)

    def ag_wait(n, half, slot, part):
        there = ag_view(slot, half, part)
        remote(there, there, ag_s.at[half, n], ag_r.at[half, n], (ctx, xo)).wait_recv()

    def cot_view(half, part):
        return cot.at[pl.ds(half * HALF + part[0], part[1]), :]

    def ag_own(half):
        ag_send(0, half, me, PS, xo, cot_view(half, PS))
        ag_send(2, half, me, QS, up, cot_view(half, QS))
        ag_send(3, half, me, QS, dn, cot_view(half, QS))
        ag_send(1, half, me, QS, xo, cot_view(half, QS))
        ag_send(4, half, me, PS, up, cot_view(half, PS))
        ag_send(5, half, me, PS, dn, cot_view(half, PS))

    def ag_first(half):
        ag_wait(0, half, xo, PS)
        ag_send(6, half, xo, PS, up)
        ag_send(7, half, xo, PS, dn)
        ag_wait(2, half, dn, QS)
        ag_send(8, half, dn, QS, up)
        ag_send(9, half, dn, QS, xo)
        ag_wait(3, half, up, QS)
        ag_send(10, half, up, QS, xo)

    def ag_second(half):
        ag_wait(4, half, dn, PS)
        ag_send(11, half, dn, PS, up)
        ag_wait(8, half, op, QS)
        ag_send(12, half, op, QS, xo)
        ag_wait(6, half, xdn, PS)
        ag_send(13, half, xdn, PS, up)

    def ag_rest(half):
        ag_wait(1, half, xo, QS)
        ag_wait(5, half, up, PS)
        ag_wait(7, half, xup, PS)
        ag_wait(9, half, xdn, QS)
        ag_wait(10, half, xup, QS)
        ag_wait(11, half, op, PS)
        ag_wait(12, half, xop, QS)
        ag_wait(13, half, xop, PS)

    ag_own(0)
    feat_halo = remote(
        feat.at[:, pl.ds(ROWS - 16, 16), :],
        feats.at[:, pl.ds(0, 16), :],
        halo_s.at[0],
        halo_r.at[0],
        (nxt, me),
    )
    feat_halo.start()
    started.append(feat_halo)
    ag_own(1)

    def short_conv(half):
        r0 = half * HALF

        def tile(c, carry):
            lanes = pl.ds(pl.multiple_of(c * 128, 128), 128)
            kept = []
            for i in range(3):
                ext = feats[i, pl.ds(r0, HALF + 16), lanes].astype(F32)
                taps = sf[i, :, lanes].astype(F32)
                value = (
                    taps[0:1] * ext[16 : 16 + HALF]
                    + taps[1:2] * ext[15 : 15 + HALF]
                    + taps[2:3] * ext[14 : 14 + HALF]
                ).astype(BF16)
                post[i, pl.ds(r0, HALF), lanes] = value
                kept.append(value.astype(F32))
            gated[pl.ds(HALF + r0, HALF), lanes] = (kept[1] * kept[2]).astype(BF16)
            return carry

        lax.fori_loop(0, TILES, tile, 0)

    load_f.wait()
    short_conv(1)
    gated_halo = remote(
        gated.at[pl.ds(2 * HALF, HALF), :],
        gated.at[pl.ds(0, HALF), :],
        halo_s.at[1],
        halo_r.at[1],
        (nxt, me),
    )
    gated_halo.start()
    started.append(gated_halo)
    feat_halo.wait_recv()

    @pl.when(ctx == 0)
    def _():
        feats[:, 0:16, :] = jnp.zeros((3, 16, CHAN), BF16)

    short_conv(0)

    def build(vec):
        def group(g, carry):
            row = jnp.broadcast_to(vec[pl.ds(g, 1), :], (HALF, 2 * HALF))
            there = pl.ds(pl.multiple_of(g * HALF, HALF), HALF)
            toep[there, :] = pltpu.roll(row, 0, 1, stride=1, stride_axis=0).astype(BF16)
            return carry

        lax.fori_loop(0, GROUPS, group, 0)

    lane_group = lax.broadcasted_iota(jnp.int32, (HALF, 128), 1) // 16

    def long_conv(window, c):
        block = toep[pl.ds(pl.multiple_of(c * PER * HALF, PER * HALF), PER * HALF), :]
        whole = dot(block, window)
        out = whole[0:HALF]
        for q in range(1, PER):
            out = jnp.where(lane_group == q, whole[q * HALF : (q + 1) * HALF], out)
        return out

    def forward_conv(half):
        r0 = half * HALF

        def tile(c, carry):
            lanes = pl.ds(pl.multiple_of(c * 128, 128), 128)
            out = long_conv(gated[pl.ds(r0, 2 * HALF), lanes], c)
            long_out[pl.ds(r0, HALF), lanes] = out
            mixer[pl.ds(r0, HALF), lanes] = (
                post[0, pl.ds(r0, HALF), lanes].astype(F32) * out
            ).astype(BF16)
            return carry

        lax.fori_loop(0, TILES, tile, 0)

    build(vec_a)
    ag_first(0)
    forward_conv(1)
    ag_second(0)
    ag_first(1)

    def project(half, side, place, owner):
        cols = pl.ds(pl.multiple_of(owner * OUT, OUT), OUT)
        part = dot(mixer[pl.ds(half * HALF, HALF), :], w[:, cols]).astype(BF16)
        psum_q[half, side, place] = part[0:QR]
        psum_p[half, place, side] = part[QR:HALF]

    def rs_copy(n, half, src, dst, dev):
        return remote(src, dst, rs_s.at[half, n], rs_r.at[half, n], (ctx, dev))

    def rs_all(half):
        copies = [
            rs_copy(0, half, psum_p.at[half, 3], in_up.at[half], up),
            rs_copy(1, half, psum_p.at[half, 2], in_own_up.at[half], dn),
            rs_copy(2, half, psum_q.at[half, 1, 3], in_q.at[half, 3], xo),
            rs_copy(3, half, psum_q.at[half, 1, 2], in_q.at[half, 2], xo),
            rs_copy(4, half, psum_q.at[half, 1, 1], in_q.at[half, 1], xo),
            rs_copy(5, half, psum_q.at[half, 1, 0], in_q.at[half, 0], xo),
            rs_copy(6, half, psum_p.at[half, 1], in_own_dn.at[half], up),
            rs_copy(7, half, psum_q.at[half, 0, 3], in_q_up.at[half], up),
            rs_copy(8, half, psum_q.at[half, 0, 2], in_q_own_up.at[half], dn),
            rs_copy(9, half, psum_q.at[half, 0, 1], in_q_own_dn.at[half], up),
            rs_copy(10, half, psum_p.at[half, 0, 1], in_x.at[half], xo),
        ]
        return copies

    rs = [rs_all(0), rs_all(1)]

    def rs_start(half, n):
        rs[half][n].start()
        started.append(rs[half][n])

    def rs_begin(half):
        project(half, 1, 3, xop)
        rs_start(half, 2)
        project(half, 0, 3, op)
        rs_start(half, 0)
        project(half, 1, 2, xdn)
        rs_start(half, 3)
        project(half, 0, 2, dn)
        rs_start(half, 1)
        project(half, 1, 1, xup)
        rs_start(half, 4)
        project(half, 1, 0, xo)
        rs_start(half, 5)
        project(half, 0, 1, up)
        project(half, 0, 0, me)

    def add(a, *others):
        total = a.astype(F32)
        for other in others:
            total = total + other.astype(F32)
        return total.astype(BF16)

    def rs_first(half):
        rs[half][2].wait_recv()
        psum_q[half, 0, 3] = add(psum_q[half, 0, 3], in_q[half, 3])
        rs_start(half, 7)
        rs[half][0].wait_recv()
        psum_p[half, 1] = add(psum_p[half, 1], in_up[half])
        rs_start(half, 6)
        rs[half][3].wait_recv()
        psum_q[half, 0, 2] = add(psum_q[half, 0, 2], in_q[half, 2])
        rs_start(half, 8)

    def rs_second(half):
        rs[half][4].wait_recv()
        rs[half][7].wait_recv()
        psum_q[half, 0, 1] = add(psum_q[half, 0, 1], in_q[half, 1], in_q_up[half])
        rs_start(half, 9)
        rs[half][1].wait_recv()
        rs[half][6].wait_recv()
        psum_p[half, 0, 1] = add(psum_p[half, 0, 1], in_own_dn[half, 1], in_own_up[half, 1])
        rs_start(half, 10)

    def rs_last(half):
        rs[half][5].wait_recv()
        rs[half][8].wait_recv()
        rs[half][9].wait_recv()
        out_mixed[pl.ds(half * HALF, QR), :] = add(
            psum_q[half, 0, 0], in_q[half, 0], in_q_own_dn[half], in_q_own_up[half]
        )
        rs[half][10].wait_recv()
        out_mixed[pl.ds(half * HALF + QR, PR), :] = add(
            psum_p[half, 0, 0], in_own_dn[half, 0], in_own_up[half, 0], in_x[half]
        )

    load_w.wait()
    rs_begin(1)
    gated_halo.wait_recv()

    @pl.when(ctx == 0)
    def _():
        gated[0:HALF, :] = jnp.zeros((HALF, CHAN), BF16)

    forward_conv(0)
    ag_second(1)
    rs_first(1)
    rs_begin(0)
    build(vec_b)

    def d_mixer(half):
        r0 = half * HALF

        def tile(c, carry):
            chans = pl.ds(pl.multiple_of(c * 256, 256), 256)
            total = jnp.zeros((HALF, 256), F32)
            for s in range(N_TP):
                total = total + dot(
                    gath[s, pl.ds(r0, HALF), :],
                    w[chans, pl.ds(s * OUT, OUT)],
                    ((1,), (1,)),
                )
            grad = total.astype(BF16).astype(F32)
            d_post[0, pl.ds(r0, HALF), chans] = grad * long_out[pl.ds(r0, HALF), chans]
            d_long[pl.ds(r0, HALF), chans] = (
                grad * post[0, pl.ds(r0, HALF), chans].astype(F32)
            ).astype(BF16)
            return carry

        lax.fori_loop(0, CHAN // 256, tile, 0)

    load_c.wait()
    ag_rest(0)
    d_mixer(0)
    long_halo = remote(
        d_long.at[pl.ds(0, HALF), :],
        d_long.at[pl.ds(2 * HALF, HALF), :],
        halo_s.at[2],
        halo_r.at[2],
        (prv, me),
    )
    long_halo.start()
    started.append(long_halo)
    rs_second(1)
    rs_first(0)
    ag_rest(1)
    d_mixer(1)

    back_rows = lax.broadcasted_iota(jnp.int32, (HALF, HALF), 0)
    back_cols = lax.broadcasted_iota(jnp.int32, (HALF, HALF), 1)
    reverse = (back_cols == HALF - 1 - back_rows).astype(BF16)
    wide_group = lax.rem(lax.broadcasted_iota(jnp.int32, (HALF, 256), 1), 128) // 16

    def corr_tile(c, carry):
        lanes = pl.ds(pl.multiple_of(c * 128, 128), 128)
        grads = jnp.concatenate(
            [d_long[pl.ds(0, HALF), lanes], d_long[pl.ds(HALF, HALF), lanes]], axis=1
        )
        grads = dot(reverse, grads)
        window = jnp.concatenate(
            [gated[pl.ds(0, 2 * HALF), lanes], gated[pl.ds(HALF, 2 * HALF), lanes]], axis=1
        )
        stack = jnp.concatenate(
            [jnp.where(wide_group == q, grads, 0.0).astype(BF16) for q in range(PER)], axis=0
        )
        whole = dot(stack, window, ((1,), (1,)))
        sums = []
        for q in range(PER):
            rolled = pltpu.roll(
                whole[q * HALF : (q + 1) * HALF], HALF + 1, 1, stride=1, stride_axis=0
            )
            sums.append(jnp.sum(rolled, axis=0, keepdims=True))
        corr[pl.ds(pl.multiple_of(c * PER, PER), PER), :] = jnp.concatenate(sums, axis=0)
        return carry

    lax.fori_loop(0, TILES, corr_tile, 0)
    fpart[...] = lax.dot_general(
        corr[...],
        (cols_i == HALF - rows_i).astype(F32),
        (((1,), (1,)), ((), ())),
        preferred_element_type=F32,
        precision=lax.Precision.HIGHEST,
    ).reshape(2, GROUPS // 2, HALF)
    sibling = (ctx + 1 - 2 * core, me)
    f_core = remote(fpart.at[1 - core], fcore, fg_s.at[0], fg_r.at[0], sibling)
    f_core.start()
    started.append(f_core)

    def backward_conv(half):
        r0 = half * HALF

        def tile(c, carry):
            lanes = pl.ds(pl.multiple_of(c * 128, 128), 128)
            out = long_conv(d_long[pl.ds(r0, 2 * HALF), lanes], c)
            for i in (1, 2):
                d_post[i, pl.ds(r0, HALF), lanes] = out * post[
                    3 - i, pl.ds(r0, HALF), lanes
                ].astype(F32)
            return carry

        lax.fori_loop(0, TILES, tile, 0)

    backward_conv(0)
    post_halo = remote(
        d_post.at[:, pl.ds(0, 8), :],
        d_post.at[:, pl.ds(ROWS, 8), :],
        halo_s.at[3],
        halo_r.at[3],
        (prv, me),
    )
    post_halo.start()
    started.append(post_halo)

    f_core.wait_recv()
    fsum[...] = fpart[core] + fcore[...]
    f_all = []
    for i in range(1, CHIPS):
        copy = remote(
            fsum,
            fall.at[chip],
            fg_s.at[i],
            fg_r.at[i],
            (2 * lax.rem(chip + i, CHIPS) + core, me),
        )
        copy.start()
        started.append(copy)

    rs_second(0)
    long_halo.wait_recv()

    @pl.when(ctx == N_CTX - 1)
    def _():
        d_long[2 * HALF : 3 * HALF, :] = jnp.zeros((HALF, CHAN), BF16)

    backward_conv(1)
    post_halo.wait_recv()

    @pl.when(ctx == N_CTX - 1)
    def _():
        d_post[:, ROWS : ROWS + 8, :] = jnp.zeros((3, 8, CHAN), F32)

    def short_back(half):
        r0 = half * HALF

        def tile(c, carry):
            lanes = pl.ds(pl.multiple_of(c * 128, 128), 128)
            for i in range(3):
                ext = d_post[i, pl.ds(r0, HALF + 8), lanes]
                taps = sf[i, :, lanes].astype(F32)
                out_grads[i, pl.ds(r0, HALF), lanes] = (
                    taps[0:1] * ext[0:HALF]
                    + taps[1:2] * ext[1 : 1 + HALF]
                    + taps[2:3] * ext[2 : 2 + HALF]
                ).astype(BF16)
            return carry

        lax.fori_loop(0, TILES, tile, 0)

    short_back(0)
    short_back(1)
    store_g = pltpu.make_async_copy(out_grads, fgrads, lsem.at[3])
    store_g.start()

    total = fsum[...]
    for i in range(1, CHIPS):
        slot = lax.rem(chip + CHIPS - i, CHIPS)
        remote(fsum, fall.at[slot], fg_s.at[i], fg_r.at[i], sibling).wait_recv()
        total = total + fall[slot]
    fout[core] = total * ((N_CTX * ROWS * 16) ** -0.5)
    f_out = remote(fout.at[core], fout.at[core], fg_s.at[16], fg_r.at[16], sibling)
    f_out.start()
    started.append(f_out)

    rs_last(1)
    rs_last(0)
    store_m = pltpu.make_async_copy(out_mixed, mixed, lsem.at[4])
    store_m.start()
    remote(
        fout.at[1 - core], fout.at[1 - core], fg_s.at[16], fg_r.at[16], sibling
    ).wait_recv()
    filt[...] = fout[...].reshape(GROUPS, HALF)

    for copy in started:
        copy.wait_send()
    store_g.wait()
    store_m.wait()


def on_device(features, short_filter, long_filter, out_weight, out_cotangent):
    hbm = pl.BlockSpec(memory_space=pl.ANY)
    vmem = pl.BlockSpec(memory_space=pltpu.VMEM)
    dma = pltpu.SemaphoreType.DMA
    scratch = [
        pltpu.VMEM((3, ROWS + 16, CHAN), BF16),
        pltpu.VMEM((3, ROWS, CHAN), BF16),
        pltpu.VMEM((ROWS + HALF, CHAN), BF16),
        pltpu.VMEM((ROWS, CHAN), F32),
        pltpu.VMEM((ROWS, CHAN), BF16),
        pltpu.VMEM((GROUPS * HALF, 2 * HALF), BF16),
        pltpu.VMEM((GROUPS, 2 * HALF), F32),
        pltpu.VMEM((GROUPS, 2 * HALF), F32),
        pltpu.VMEM((N_TP, ROWS, OUT), BF16),
        pltpu.VMEM((CHAN, N_TP * OUT), BF16),
        pltpu.VMEM((2, 4, 2, PR, OUT), BF16),
        pltpu.VMEM((2, 2, 4, QR, OUT), BF16),
        pltpu.VMEM((2, 2, PR, OUT), BF16),
        pltpu.VMEM((2, 2, PR, OUT), BF16),
        pltpu.VMEM((2, 2, PR, OUT), BF16),
        pltpu.VMEM((2, PR, OUT), BF16),
        pltpu.VMEM((2, 4, QR, OUT), BF16),
        pltpu.VMEM((2, QR, OUT), BF16),
        pltpu.VMEM((2, QR, OUT), BF16),
        pltpu.VMEM((2, QR, OUT), BF16),
        pltpu.VMEM((ROWS + HALF, CHAN), BF16),
        pltpu.VMEM((3, ROWS + 8, CHAN), F32),
        pltpu.VMEM((GROUPS, 2 * HALF), F32),
        pltpu.VMEM((2, GROUPS // 2, HALF), F32),
        pltpu.VMEM((GROUPS // 2, HALF), F32),
        pltpu.VMEM((GROUPS // 2, HALF), F32),
        pltpu.VMEM((CHIPS, GROUPS // 2, HALF), F32),
        pltpu.VMEM((2, GROUPS // 2, HALF), F32),
        pltpu.VMEM((ROWS, OUT), BF16),
        pltpu.VMEM((3, ROWS, CHAN), BF16),
        dma((5,)),
        dma((2, 14)),
        dma((2, 14)),
        dma((2, 11)),
        dma((2, 11)),
        dma((4,)),
        dma((4,)),
        dma((17,)),
        dma((17,)),
    ]
    return pl.pallas_call(
        kernel,
        out_shape=(
            jax.ShapeDtypeStruct((ROWS, OUT), BF16),
            jax.ShapeDtypeStruct((3, ROWS, CHAN), BF16),
            jax.ShapeDtypeStruct((GROUPS, HALF), F32),
        ),
        in_specs=[hbm, vmem, vmem, hbm, hbm],
        out_specs=(hbm, hbm, vmem),
        scratch_shapes=scratch,
        compiler_params=pltpu.CompilerParams(
            collective_id=0, has_side_effects=True, vmem_limit_bytes=56 * 2**20
        ),
    )(features, short_filter, long_filter, out_weight, out_cotangent)


def solution(mesh):
    placed = (
        P(None, "ctx", "tp"),
        P(None, None, "tp"),
        P("tp", None),
        P("tp", None),
        P("ctx", "tp"),
    )
    return jax.shard_map(
        on_device,
        mesh=mesh,
        in_specs=placed,
        out_specs=(P("ctx", "tp"), P(None, "ctx", "tp"), P("tp", None)),
        check_vma=False,
    )
```

```python
import functools

import jax
import jax.numpy as jnp
from jax import lax
from jax.experimental import pallas as pl
from jax.experimental.pallas import tpu as pltpu
from jax.sharding import PartitionSpec as P

MESH = pl.DeviceIdType.MESH
F32 = jnp.float32
BF16 = jnp.bfloat16
ROWS = 256
HALF = 128
CHAN = 1024
OUT = 512
N_TP = 8
N_CTX = 32
GROUPS = 64
QR = 48
PR = HALF - QR
TILES = CHAN // 128
PER = 8
QUAD = 4
RINGS = N_CTX // QUAD
SHARE = GROUPS // QUAD
STEP = 16
SPAN = HALF + STEP
STEPS = HALF // STEP


def dot(a, b, dims=((1,), (0,))):
    return lax.dot_general(a, b, (dims, ((), ())), preferred_element_type=F32)


def kernel(
    feat,
    sf,
    lf,
    w_hbm,
    cot,
    mixed,
    fgrads,
    filt,
    feats,
    post,
    gated,
    long_out,
    mixer,
    toep_a,
    toep_b,
    vec_a,
    vec_b,
    gath,
    w,
    psum_p,
    psum_q,
    in_up,
    in_own_dn,
    in_own_up,
    in_x,
    in_q,
    in_q_up,
    in_q_own_dn,
    in_q_own_up,
    d_long,
    d_post,
    corr_lo,
    corr_hi,
    d_acc,
    fpart,
    fcore,
    fsum,
    fall,
    fout,
    out_mixed,
    out_grads,
    lsem,
    ag_s,
    ag_r,
    rs_s,
    rs_r,
    halo_s,
    halo_r,
    fg_s,
    fg_r,
):
    ctx = lax.axis_index("ctx")
    me = lax.axis_index("tp")
    core = lax.rem(ctx, 2)
    quad = lax.rem(ctx, QUAD)
    ring = ctx // QUAD
    corner = ctx - quad
    xl = me // 4
    yl = lax.rem(me, 4)
    step = 1 + 2 * core
    back = 3 - 2 * core
    y_up = lax.rem(yl + step, 4)
    y_dn = lax.rem(yl + back, 4)
    y_op = lax.rem(yl + 2, 4)
    own_base = xl * 4
    x_base = 4 - xl * 4
    up = own_base + y_up
    dn = own_base + y_dn
    op = own_base + y_op
    xo = x_base + yl
    xup = x_base + y_up
    xdn = x_base + y_dn
    xop = x_base + y_op
    nxt = lax.rem(ctx + 1, N_CTX)
    prv = lax.rem(ctx + N_CTX - 1, N_CTX)

    load_f = pltpu.make_async_copy(feat, feats.at[:, pl.ds(16, ROWS), :], lsem.at[0])
    load_w = pltpu.make_async_copy(w_hbm, w, lsem.at[1])
    load_c = pltpu.make_async_copy(cot, gath.at[me], lsem.at[2])
    load_f.start()
    load_w.start()
    load_c.start()

    barrier = pltpu.get_barrier_semaphore()
    across = core * nxt + (1 - core) * prv
    quads = [corner + lax.rem(quad + k, QUAD) for k in range(1, QUAD)]
    along = [lax.rem(ring + k, RINGS) * QUAD + quad for k in range(1, RINGS)]
    peers = [(ctx, xo), (ctx, up), (ctx, dn), (across, me)]
    peers += [(dev, me) for dev in quads + along]
    for peer in peers:
        pl.semaphore_signal(barrier, inc=1, device_id=peer, device_id_type=MESH)

    rows_i = lax.broadcasted_iota(jnp.int32, (HALF, 2 * HALF), 0)
    cols_i = lax.broadcasted_iota(jnp.int32, (HALF, 2 * HALF), 1)
    flip = (cols_i == HALF - rows_i).astype(BF16)
    keep = (cols_i == rows_i).astype(BF16)
    vec_a[...] = dot(lf[...], flip)
    vec_b[...] = dot(lf[...], keep)

    def build(vec, toep):
        def group(g, carry):
            row = jnp.broadcast_to(vec[pl.ds(g, 1), :], (STEP, 2 * HALF))
            there = pl.ds(pl.multiple_of(g * STEP, STEP), STEP)
            toep[there, :] = pltpu.roll(row, 0, 1, stride=1, stride_axis=0).astype(BF16)
            return carry

        lax.fori_loop(0, GROUPS, group, 0, unroll=8)

    build(vec_a, toep_a)
    pl.semaphore_wait(barrier, len(peers))

    started = []

    def remote(src, dst, send, recv, dev):
        return pltpu.make_async_remote_copy(
            src_ref=src,
            dst_ref=dst,
            send_sem=send,
            recv_sem=recv,
            device_id=dev,
            device_id_type=MESH,
        )

    QS = (0, QR)
    PS = (QR, PR)

    def ag_view(slot, half, part):
        return gath.at[slot, pl.ds(half * HALF + part[0], part[1]), :]

    def ag_send(n, half, slot, part, dev, src=None):
        there = ag_view(slot, half, part)
        copy = remote(
            there if src is None else src,
            there,
            ag_s.at[half, n],
            ag_r.at[half, n],
            (ctx, dev),
        )
        copy.start()
        started.append(copy)

    def ag_wait(n, half, slot, part):
        there = ag_view(slot, half, part)
        remote(there, there, ag_s.at[half, n], ag_r.at[half, n], (ctx, xo)).wait_recv()

    def cot_view(half, part):
        return cot.at[pl.ds(half * HALF + part[0], part[1]), :]

    def ag_own(half):
        ag_send(0, half, me, PS, xo, cot_view(half, PS))
        ag_send(2, half, me, QS, up, cot_view(half, QS))
        ag_send(3, half, me, QS, dn, cot_view(half, QS))
        ag_send(1, half, me, QS, xo, cot_view(half, QS))
        ag_send(4, half, me, PS, up, cot_view(half, PS))
        ag_send(5, half, me, PS, dn, cot_view(half, PS))

    def ag_first(half):
        ag_wait(2, half, dn, QS)
        ag_send(8, half, dn, QS, up)
        ag_send(9, half, dn, QS, xo)
        ag_wait(3, half, up, QS)
        ag_send(10, half, up, QS, xo)
        ag_wait(0, half, xo, PS)
        ag_send(6, half, xo, PS, up)
        ag_send(7, half, xo, PS, dn)

    def ag_second(half):
        ag_wait(4, half, dn, PS)
        ag_send(11, half, dn, PS, up)

    def ag_third(half):
        ag_wait(8, half, op, QS)
        ag_send(12, half, op, QS, xo)
        ag_wait(6, half, xdn, PS)
        ag_send(13, half, xdn, PS, up)

    def ag_near(half):
        ag_wait(1, half, xo, QS)
        ag_wait(5, half, up, PS)

    def ag_rest(half):
        ag_wait(7, half, xup, PS)
        ag_wait(9, half, xdn, QS)
        ag_wait(10, half, xup, QS)
        ag_wait(11, half, op, PS)
        ag_wait(12, half, xop, QS)
        ag_wait(13, half, xop, PS)

    feat_halo = remote(
        feat.at[:, pl.ds(ROWS - 16, 16), :],
        feats.at[:, pl.ds(0, 16), :],
        halo_s.at[0],
        halo_r.at[0],
        (nxt, me),
    )
    feat_halo.start()
    started.append(feat_halo)
    ag_own(0)

    def short_conv(half):
        r0 = half * HALF

        def tile(c, carry):
            lanes = pl.ds(pl.multiple_of(c * 128, 128), 128)
            kept = []
            for i in range(3):
                ext = feats[i, pl.ds(r0, HALF + 16), lanes].astype(F32)
                taps = sf[i, :, lanes].astype(F32)
                value = (
                    taps[0:1] * ext[16 : 16 + HALF]
                    + taps[1:2] * ext[15 : 15 + HALF]
                    + taps[2:3] * ext[14 : 14 + HALF]
                ).astype(BF16)
                post[i, pl.ds(r0, HALF), lanes] = value
                kept.append(value.astype(F32))
            gated[pl.ds(HALF + r0, HALF), lanes] = (kept[1] * kept[2]).astype(BF16)
            return carry

        lax.fori_loop(0, TILES, tile, 0, unroll=True)

    load_f.wait()
    short_conv(1)
    gated_halo = remote(
        gated.at[pl.ds(2 * HALF, HALF), :],
        gated.at[pl.ds(0, HALF), :],
        halo_s.at[1],
        halo_r.at[1],
        (nxt, me),
    )
    gated_halo.start()
    started.append(gated_halo)
    ag_own(1)
    build(vec_b, toep_b)
    ag_first(0)
    feat_halo.wait_recv()

    @pl.when(ctx == 0)
    def _():
        feats[:, 0:16, :] = jnp.zeros((3, 16, CHAN), BF16)

    short_conv(0)
    ag_second(0)

    lane_group = lax.broadcasted_iota(jnp.int32, (STEP, 128), 1) // 16

    def long_conv(toep, source, r0, c, lanes):
        block = toep[pl.ds(pl.multiple_of(c * HALF, HALF), HALF), 0:SPAN]
        window = jnp.concatenate(
            [source[pl.ds(r0 + STEP * a, SPAN), lanes] for a in range(STEPS)], axis=1
        )
        whole = dot(block, window)
        outs = []
        for a in range(STEPS):
            cols = slice(a * 128, (a + 1) * 128)
            out = whole[0:STEP, cols]
            for q in range(1, PER):
                out = jnp.where(lane_group == q, whole[q * STEP : (q + 1) * STEP, cols], out)
            outs.append(out)
        return jnp.concatenate(outs, axis=0)

    def forward_conv(half):
        r0 = half * HALF

        def tile(c, carry):
            lanes = pl.ds(pl.multiple_of(c * 128, 128), 128)
            out = long_conv(toep_a, gated, r0, c, lanes)
            long_out[pl.ds(r0, HALF), lanes] = out
            mixer[pl.ds(r0, HALF), lanes] = (
                post[0, pl.ds(r0, HALF), lanes].astype(F32) * out
            ).astype(BF16)
            return carry

        lax.fori_loop(0, TILES, tile, 0, unroll=True)

    forward_conv(1)

    def project(half, side, place, owner):
        cols = pl.ds(pl.multiple_of(owner * OUT, OUT), OUT)
        part = dot(mixer[pl.ds(half * HALF, HALF), :], w[:, cols]).astype(BF16)
        psum_q[half, side, place] = part[0:QR]
        psum_p[half, place, side] = part[QR:HALF]

    def rs_copy(n, half, src, dst, dev):
        return remote(src, dst, rs_s.at[half, n], rs_r.at[half, n], (ctx, dev))

    def rs_all(half):
        copies = [
            rs_copy(0, half, psum_p.at[half, 3], in_up.at[half], up),
            rs_copy(1, half, psum_p.at[half, 2], in_own_up.at[half], dn),
            rs_copy(2, half, psum_q.at[half, 1, 3], in_q.at[half, 3], xo),
            rs_copy(3, half, psum_q.at[half, 1, 2], in_q.at[half, 2], xo),
            rs_copy(4, half, psum_q.at[half, 1, 1], in_q.at[half, 1], xo),
            rs_copy(5, half, psum_q.at[half, 1, 0], in_q.at[half, 0], xo),
            rs_copy(6, half, psum_p.at[half, 1], in_own_dn.at[half], up),
            rs_copy(7, half, psum_q.at[half, 0, 3], in_q_up.at[half], up),
            rs_copy(8, half, psum_q.at[half, 0, 2], in_q_own_up.at[half], dn),
            rs_copy(9, half, psum_q.at[half, 0, 1], in_q_own_dn.at[half], up),
            rs_copy(10, half, psum_p.at[half, 0, 1], in_x.at[half], xo),
        ]
        return copies

    rs = [rs_all(0), rs_all(1)]

    def rs_start(half, n):
        rs[half][n].start()
        started.append(rs[half][n])

    def project_all(half):
        project(half, 1, 3, xop)
        project(half, 0, 3, op)
        project(half, 1, 2, xdn)
        project(half, 0, 2, dn)
        project(half, 1, 1, xup)
        project(half, 1, 0, xo)
        project(half, 0, 1, up)
        project(half, 0, 0, me)

    def rs_begin(half):
        for n in (2, 0, 3, 1, 4, 5):
            rs_start(half, n)

    def add(a, *others):
        total = a.astype(F32)
        for other in others:
            total = total + other.astype(F32)
        return total.astype(BF16)

    def rs_first(half):
        rs[half][2].wait_recv()
        psum_q[half, 0, 3] = add(psum_q[half, 0, 3], in_q[half, 3])
        rs_start(half, 7)
        rs[half][0].wait_recv()
        psum_p[half, 1] = add(psum_p[half, 1], in_up[half])
        rs_start(half, 6)
        rs[half][3].wait_recv()
        psum_q[half, 0, 2] = add(psum_q[half, 0, 2], in_q[half, 2])
        rs_start(half, 8)

    def rs_second(half):
        rs[half][4].wait_recv()
        rs[half][7].wait_recv()
        psum_q[half, 0, 1] = add(psum_q[half, 0, 1], in_q[half, 1], in_q_up[half])
        rs_start(half, 9)
        rs[half][1].wait_recv()
        rs[half][6].wait_recv()
        psum_p[half, 0, 1] = add(psum_p[half, 0, 1], in_own_dn[half, 1], in_own_up[half, 1])
        rs_start(half, 10)

    def rs_last(half):
        rs[half][5].wait_recv()
        rs[half][8].wait_recv()
        rs[half][9].wait_recv()
        out_mixed[pl.ds(half * HALF, QR), :] = add(
            psum_q[half, 0, 0], in_q[half, 0], in_q_own_dn[half], in_q_own_up[half]
        )
        rs[half][10].wait_recv()
        out_mixed[pl.ds(half * HALF + QR, PR), :] = add(
            psum_p[half, 0, 0], in_own_dn[half, 0], in_own_up[half, 0], in_x[half]
        )

    load_w.wait()
    project_all(1)
    ag_third(0)
    ag_first(1)
    gated_halo.wait_recv()

    @pl.when(ctx == 0)
    def _():
        gated[0:HALF, :] = jnp.zeros((HALF, CHAN), BF16)

    forward_conv(0)
    ag_second(1)
    project_all(0)
    rs_begin(1)
    ag_third(1)
    rs_begin(0)

    def d_mixer(half, slots, first, last):
        r0 = half * HALF
        for c in range(CHAN // 256):
            chans = pl.ds(c * 256, 256)
            total = None if first else d_acc[chans, :]
            for s in slots:
                cols = pl.ds(pl.multiple_of(s * OUT, OUT), OUT)
                part = dot(w[chans, cols], gath[s, pl.ds(r0, HALF), :], ((1,), (1,)))
                total = part if total is None else total + part
            if not last:
                d_acc[chans, :] = total
                continue
            grad = total.T.astype(BF16).astype(F32)
            d_post[0, pl.ds(r0, HALF), chans] = grad * long_out[pl.ds(r0, HALF), chans]
            d_long[pl.ds(r0, HALF), chans] = (
                grad * post[0, pl.ds(r0, HALF), chans].astype(F32)
            ).astype(BF16)

    load_c.wait()
    ag_near(0)
    ag_rest(0)
    d_mixer(0, range(N_TP), True, True)
    long_halo = remote(
        d_long.at[pl.ds(0, HALF), :],
        d_long.at[pl.ds(2 * HALF, HALF), :],
        halo_s.at[2],
        halo_r.at[2],
        (prv, me),
    )
    long_halo.start()
    started.append(long_halo)
    rs_first(1)

    wide_group = lax.rem(lax.broadcasted_iota(jnp.int32, (STEP, CHAN), 1), 128) // 16

    def correlate(half):
        r0 = half * HALF
        for c in range(TILES):
            lanes = pl.ds(c * 128, 128)
            grads = jnp.concatenate(
                [d_long[pl.ds(r0 + STEP * a, STEP), lanes] for a in range(STEPS)], axis=1
            )
            stack = jnp.concatenate(
                [jnp.where(wide_group == q, grads, jnp.zeros_like(grads)) for q in range(PER)],
                axis=0,
            )
            window = jnp.concatenate(
                [gated[pl.ds(r0 + STEP * a, SPAN), lanes] for a in range(STEPS)], axis=1
            )
            whole = dot(stack, window, ((1,), (1,)))
            there = pl.ds(c * HALF, HALF)
            if half == 0:
                corr_lo[there, :] = whole[:, 0:128]
                corr_hi[there, 0:STEP] = whole[:, 128:SPAN]
            else:
                corr_lo[there, :] = corr_lo[there, :] + whole[:, 0:128]
                corr_hi[there, 0:STEP] = corr_hi[there, 0:STEP] + whole[:, 128:SPAN]

    def corr_row(b):
        rows = pl.ds(b, GROUPS, stride=STEP)
        return jnp.concatenate([corr_lo[rows, :], corr_hi[rows, :]], axis=1)

    ag_near(1)
    d_mixer(1, (me, xo, up, dn), True, False)
    rs_first(0)
    correlate(0)
    ag_rest(1)
    d_mixer(1, (xup, xdn, op, xop), False, True)
    correlate(1)
    taps_sum = corr_row(0)
    for b in range(1, STEP):
        taps_sum = taps_sum + pltpu.roll(corr_row(b), 2 * HALF - b, 1)
    lane_i = lax.broadcasted_iota(jnp.int32, (GROUPS, 2 * HALF), 1)
    taps_sum = jnp.where((lane_i >= 1) & (lane_i <= HALF), taps_sum, 0.0)
    fpart[...] = lax.dot_general(
        taps_sum,
        (cols_i == HALF - rows_i).astype(F32),
        (((1,), (1,)), ((), ())),
        preferred_element_type=F32,
        precision=lax.Precision.HIGHEST,
    ).reshape(QUAD, SHARE, HALF)
    for k in range(1, QUAD):
        there = lax.rem(quad + k, QUAD)
        copy = remote(
            fpart.at[there], fcore.at[quad], fg_s.at[k], fg_r.at[k], (quads[k - 1], me)
        )
        copy.start()
        started.append(copy)
    rs_second(1)

    def backward_conv(half):
        r0 = half * HALF

        def tile(c, carry):
            lanes = pl.ds(pl.multiple_of(c * 128, 128), 128)
            out = long_conv(toep_b, d_long, r0, c, lanes)
            for i in (1, 2):
                d_post[i, pl.ds(r0, HALF), lanes] = out * post[
                    3 - i, pl.ds(r0, HALF), lanes
                ].astype(F32)
            return carry

        lax.fori_loop(0, TILES, tile, 0, unroll=True)

    backward_conv(0)
    post_halo = remote(
        d_post.at[:, pl.ds(0, 8), :],
        d_post.at[:, pl.ds(ROWS, 8), :],
        halo_s.at[3],
        halo_r.at[3],
        (prv, me),
    )
    post_halo.start()
    started.append(post_halo)

    own_sum = fpart[quad]
    for k in range(1, QUAD):
        slot = lax.rem(quad + QUAD - k, QUAD)
        here = fcore.at[slot]
        remote(here, here, fg_s.at[k], fg_r.at[k], (quads[k - 1], me)).wait_recv()
        own_sum = own_sum + fcore[slot]
    fsum[...] = own_sum
    for k in range(1, RINGS):
        copy = remote(
            fsum, fall.at[ring], fg_s.at[3 + k], fg_r.at[3 + k], (along[k - 1], me)
        )
        copy.start()
        started.append(copy)

    rs_second(0)
    long_halo.wait_recv()

    @pl.when(ctx == N_CTX - 1)
    def _():
        d_long[2 * HALF : 3 * HALF, :] = jnp.zeros((HALF, CHAN), BF16)

    backward_conv(1)
    post_halo.wait_recv()

    @pl.when(ctx == N_CTX - 1)
    def _():
        d_post[:, ROWS : ROWS + 8, :] = jnp.zeros((3, 8, CHAN), F32)

    def short_back(half):
        r0 = half * HALF

        def tile(c, carry):
            lanes = pl.ds(pl.multiple_of(c * 128, 128), 128)
            for i in range(3):
                ext = d_post[i, pl.ds(r0, HALF + 8), lanes]
                taps = sf[i, :, lanes].astype(F32)
                out_grads[i, pl.ds(r0, HALF), lanes] = (
                    taps[0:1] * ext[0:HALF]
                    + taps[1:2] * ext[1 : 1 + HALF]
                    + taps[2:3] * ext[2 : 2 + HALF]
                ).astype(BF16)
            return carry

        lax.fori_loop(0, TILES, tile, 0, unroll=True)

    short_back(0)
    short_back(1)
    store_g = pltpu.make_async_copy(out_grads, fgrads, lsem.at[3])
    store_g.start()

    total = fsum[...]
    for k in range(1, RINGS):
        slot = lax.rem(ring + RINGS - k, RINGS)
        here = fall.at[slot]
        remote(here, here, fg_s.at[3 + k], fg_r.at[3 + k], (along[k - 1], me)).wait_recv()
        total = total + fall[slot]
    fout[quad] = total * ((N_CTX * ROWS * 16) ** -0.5)
    for k in range(1, QUAD):
        here = fout.at[quad]
        copy = remote(here, here, fg_s.at[10 + k], fg_r.at[10 + k], (quads[k - 1], me))
        copy.start()
        started.append(copy)

    rs_last(1)
    rs_last(0)
    store_m = pltpu.make_async_copy(out_mixed, mixed, lsem.at[4])
    store_m.start()
    for k in range(1, QUAD):
        here = fout.at[lax.rem(quad + QUAD - k, QUAD)]
        remote(here, here, fg_s.at[10 + k], fg_r.at[10 + k], (quads[k - 1], me)).wait_recv()
    filt[...] = fout[...].reshape(GROUPS, HALF)

    for copy in started:
        copy.wait_send()
    store_g.wait()
    store_m.wait()


def publish(mixed, fgrads, filt, out_mixed, out_fgrads, out_filt, sem):
    copies = [
        pltpu.make_async_copy(fgrads, out_fgrads, sem.at[0]),
        pltpu.make_async_copy(mixed, out_mixed, sem.at[1]),
        pltpu.make_async_copy(filt, out_filt, sem.at[2]),
    ]
    for copy in copies:
        copy.start()
    for copy in copies:
        copy.wait()


def on_device(features, short_filter, long_filter, out_weight, out_cotangent):
    hbm = pl.BlockSpec(memory_space=pl.ANY)
    vmem = pl.BlockSpec(memory_space=pltpu.VMEM)
    dma = pltpu.SemaphoreType.DMA
    scratch = [
        pltpu.VMEM((3, ROWS + 16, CHAN), BF16),
        pltpu.VMEM((3, ROWS, CHAN), BF16),
        pltpu.VMEM((ROWS + HALF, CHAN), BF16),
        pltpu.VMEM((ROWS, CHAN), F32),
        pltpu.VMEM((ROWS, CHAN), BF16),
        pltpu.VMEM((GROUPS * STEP, 2 * HALF), BF16),
        pltpu.VMEM((GROUPS * STEP, 2 * HALF), BF16),
        pltpu.VMEM((GROUPS, 2 * HALF), F32),
        pltpu.VMEM((GROUPS, 2 * HALF), F32),
        pltpu.VMEM((N_TP, ROWS, OUT), BF16),
        pltpu.VMEM((CHAN, N_TP * OUT), BF16),
        pltpu.VMEM((2, 4, 2, PR, OUT), BF16),
        pltpu.VMEM((2, 2, 4, QR, OUT), BF16),
        pltpu.VMEM((2, 2, PR, OUT), BF16),
        pltpu.VMEM((2, 2, PR, OUT), BF16),
        pltpu.VMEM((2, 2, PR, OUT), BF16),
        pltpu.VMEM((2, PR, OUT), BF16),
        pltpu.VMEM((2, 4, QR, OUT), BF16),
        pltpu.VMEM((2, QR, OUT), BF16),
        pltpu.VMEM((2, QR, OUT), BF16),
        pltpu.VMEM((2, QR, OUT), BF16),
        pltpu.VMEM((ROWS + HALF, CHAN), BF16),
        pltpu.VMEM((3, ROWS + 8, CHAN), F32),
        pltpu.VMEM((GROUPS * STEP, HALF), F32),
        pltpu.VMEM((GROUPS * STEP, HALF), F32),
        pltpu.VMEM((CHAN, HALF), F32),
        pltpu.VMEM((QUAD, SHARE, HALF), F32),
        pltpu.VMEM((QUAD, SHARE, HALF), F32),
        pltpu.VMEM((SHARE, HALF), F32),
        pltpu.VMEM((RINGS, SHARE, HALF), F32),
        pltpu.VMEM((QUAD, SHARE, HALF), F32),
        pltpu.VMEM((ROWS, OUT), BF16),
        pltpu.VMEM((3, ROWS, CHAN), BF16),
        dma((5,)),
        dma((2, 14)),
        dma((2, 14)),
        dma((2, 11)),
        dma((2, 11)),
        dma((4,)),
        dma((4,)),
        dma((14,)),
        dma((14,)),
    ]
    shapes = (
        jax.ShapeDtypeStruct((ROWS, OUT), BF16),
        jax.ShapeDtypeStruct((3, ROWS, CHAN), BF16),
        jax.ShapeDtypeStruct((GROUPS, HALF), F32),
    )
    results = pl.pallas_call(
        kernel,
        out_shape=shapes,
        in_specs=[hbm, vmem, vmem, hbm, hbm],
        out_specs=(hbm, hbm, vmem),
        scratch_shapes=scratch,
        compiler_params=pltpu.CompilerParams(
            collective_id=0, has_side_effects=True, vmem_limit_bytes=56 * 2**20
        ),
    )(features, short_filter, long_filter, out_weight, out_cotangent)
    return pl.pallas_call(
        publish,
        out_shape=shapes,
        in_specs=[vmem] * 3,
        out_specs=(hbm,) * 3,
        scratch_shapes=[dma((3,))],
    )(*results)


def solution(mesh):
    placed = (
        P(None, "ctx", "tp"),
        P(None, None, "tp"),
        P("tp", None),
        P("tp", None),
        P("ctx", "tp"),
    )
    return jax.shard_map(
        on_device,
        mesh=mesh,
        in_specs=placed,
        out_specs=(P("ctx", "tp"), P(None, "ctx", "tp"), P("tp", None)),
        check_vma=False,
    )
```

```python
import functools

import jax
import jax.numpy as jnp
from jax import lax
from jax.experimental import pallas as pl
from jax.experimental.pallas import tpu as pltpu
from jax.sharding import PartitionSpec as P

MESH = pl.DeviceIdType.MESH
F32 = jnp.float32
BF16 = jnp.bfloat16
ROWS = 256
HALF = 128
CHAN = 1024
OUT = 512
N_TP = 8
N_CTX = 32
GROUPS = 64
QR = (48, 32)
PR = (HALF - QR[0], HALF - QR[1])
QM = max(QR)
PM = max(PR)
TILES = CHAN // 128
PER = 8
QUAD = 4
RINGS = N_CTX // QUAD
SHARE = GROUPS // QUAD
STEP = 16
SPAN = HALF + STEP
STEPS = HALF // STEP


def dot(a, b, dims=((1,), (0,))):
    return lax.dot_general(a, b, (dims, ((), ())), preferred_element_type=F32)


def kernel(
    feat,
    sf,
    lf,
    w_hbm,
    cot,
    mixed,
    fgrads,
    filt,
    feats,
    post,
    gated,
    long_out,
    mixer,
    toep_a,
    toep_b,
    vec_a,
    vec_b,
    gath,
    w,
    psum_p,
    psum_q,
    in_up,
    in_own_dn,
    in_own_up,
    in_x,
    in_q,
    in_q_up,
    in_q_own_dn,
    in_q_own_up,
    d_long,
    d_post,
    corr_lo,
    corr_hi,
    d_acc,
    fpart,
    fcore,
    fsum,
    fall,
    fout,
    out_mixed,
    out_grads,
    lsem,
    ag_s,
    ag_r,
    rs_s,
    rs_r,
    halo_s,
    halo_r,
    fg_s,
    fg_r,
    far,
):
    ctx = lax.axis_index("ctx")
    me = lax.axis_index("tp")
    core = lax.rem(ctx, 2)
    quad = lax.rem(ctx, QUAD)
    ring = ctx // QUAD
    corner = ctx - quad
    xl = me // 4
    yl = lax.rem(me, 4)
    step = 1 + 2 * core
    back = 3 - 2 * core
    y_up = lax.rem(yl + step, 4)
    y_dn = lax.rem(yl + back, 4)
    y_op = lax.rem(yl + 2, 4)
    own_base = xl * 4
    x_base = 4 - xl * 4
    up = own_base + y_up
    dn = own_base + y_dn
    op = own_base + y_op
    xo = x_base + yl
    xup = x_base + y_up
    xdn = x_base + y_dn
    xop = x_base + y_op
    nxt = lax.rem(ctx + 1, N_CTX)
    prv = lax.rem(ctx + N_CTX - 1, N_CTX)

    load_f = pltpu.make_async_copy(feat, feats.at[:, pl.ds(16, ROWS), :], lsem.at[0])
    load_w = pltpu.make_async_copy(w_hbm, w, lsem.at[1])
    load_c = pltpu.make_async_copy(cot, gath.at[me], lsem.at[2])
    load_f.start()
    load_w.start()
    load_c.start()

    first = ctx == 0
    final = ctx == N_CTX - 1
    barrier = pltpu.get_barrier_semaphore()

    def greet(sem, dev):
        pl.semaphore_signal(sem, inc=1, device_id=dev, device_id_type=MESH)

    across = core * nxt + (1 - core) * prv
    quads = [corner + lax.rem(quad + k, QUAD) for k in range(1, QUAD)]
    along = [lax.rem(ring + k, RINGS) * QUAD + quad for k in range(1, RINGS)]
    for near in [(ctx, xo), (ctx, up), (ctx, dn)] + [(dev, me) for dev in quads]:
        greet(barrier, near)

    @pl.when(jnp.logical_not(first | final))
    def _():
        greet(barrier, (across, me))

    for k in range(1, RINGS):

        @pl.when(ring + k < RINGS)
        def _(k=k):
            greet(barrier, (along[k - 1], me))

    rows_i = lax.broadcasted_iota(jnp.int32, (HALF, 2 * HALF), 0)
    cols_i = lax.broadcasted_iota(jnp.int32, (HALF, 2 * HALF), 1)
    flip = (cols_i == HALF - rows_i).astype(BF16)
    keep = (cols_i == rows_i).astype(BF16)
    vec_a[...] = dot(lf[...], flip)
    vec_b[...] = dot(lf[...], keep)

    def build(vec, toep):
        def group(g, carry):
            row = jnp.broadcast_to(vec[pl.ds(g, 1), :], (STEP, 2 * HALF))
            there = pl.ds(pl.multiple_of(g * STEP, STEP), STEP)
            toep[there, :] = pltpu.roll(row, 0, 1, stride=1, stride_axis=0).astype(BF16)
            return carry

        lax.fori_loop(0, GROUPS, group, 0, unroll=8)

    build(vec_a, toep_a)
    ends = jnp.where(first | final, 0, 1)
    pl.semaphore_wait(barrier, 6 + ends + ring)

    started = []

    def remote(src, dst, send, recv, dev):
        return pltpu.make_async_remote_copy(
            src_ref=src,
            dst_ref=dst,
            send_sem=send,
            recv_sem=recv,
            device_id=dev,
            device_id_type=MESH,
        )

    QS, PS = 0, 1

    def part_rows(half, part):
        if part == QS:
            return pl.ds(half * HALF, QR[half])
        return pl.ds(half * HALF + QR[half], PR[half])

    def ag_view(slot, half, part):
        return gath.at[slot, part_rows(half, part), :]

    def ag_send(n, half, slot, part, dev, src=None):
        there = ag_view(slot, half, part)
        copy = remote(
            there if src is None else src,
            there,
            ag_s.at[half, n],
            ag_r.at[half, n],
            (ctx, dev),
        )
        copy.start()
        started.append(copy)

    def ag_wait(n, half, slot, part):
        there = ag_view(slot, half, part)
        remote(there, there, ag_s.at[half, n], ag_r.at[half, n], (ctx, xo)).wait_recv()

    def cot_view(half, part):
        return cot.at[part_rows(half, part), :]

    def own_p(half):
        ag_send(0, half, me, PS, xo, cot_view(half, PS))

    def own_q(half):
        ag_send(2, half, me, QS, up, cot_view(half, QS))
        ag_send(3, half, me, QS, dn, cot_view(half, QS))

    def own_r(half):
        ag_send(1, half, me, QS, xo, cot_view(half, QS))
        ag_send(4, half, me, PS, up, cot_view(half, PS))
        ag_send(5, half, me, PS, dn, cot_view(half, PS))

    def pass_q_dn(half):
        ag_wait(2, half, dn, QS)
        ag_send(8, half, dn, QS, up)
        ag_send(9, half, dn, QS, xo)

    def pass_q_up(half):
        ag_wait(3, half, up, QS)
        ag_send(10, half, up, QS, xo)

    def pass_p(half):
        ag_wait(0, half, xo, PS)
        ag_send(6, half, xo, PS, up)
        ag_send(7, half, xo, PS, dn)

    def pass_dn(half):
        ag_wait(4, half, dn, PS)
        ag_send(11, half, dn, PS, up)

    def pass_op(half):
        ag_wait(8, half, op, QS)
        ag_send(12, half, op, QS, xo)

    def pass_xdn(half):
        ag_wait(6, half, xdn, PS)
        ag_send(13, half, xdn, PS, up)

    def short_conv(half):
        r0 = half * HALF

        def tile(c, carry):
            lanes = pl.ds(pl.multiple_of(c * 128, 128), 128)
            kept = []
            for i in range(3):
                ext = feats[i, pl.ds(r0, HALF + 16), lanes].astype(F32)
                taps = sf[i, :, lanes].astype(F32)
                value = (
                    taps[0:1] * ext[16 : 16 + HALF]
                    + taps[1:2] * ext[15 : 15 + HALF]
                    + taps[2:3] * ext[14 : 14 + HALF]
                ).astype(BF16)
                post[i, pl.ds(r0, HALF), lanes] = value
                kept.append(value.astype(F32))
            gated[pl.ds(HALF + r0, HALF), lanes] = (kept[1] * kept[2]).astype(BF16)
            return carry

        lax.fori_loop(0, TILES, tile, 0, unroll=True)

    lane_group = lax.broadcasted_iota(jnp.int32, (STEP, 128), 1) // 16

    def long_conv(toep, source, r0, c, lanes):
        block = toep[pl.ds(pl.multiple_of(c * HALF, HALF), HALF), 0:SPAN]
        window = jnp.concatenate(
            [source[pl.ds(r0 + STEP * a, SPAN), lanes] for a in range(STEPS)], axis=1
        )
        whole = dot(block, window)
        outs = []
        for a in range(STEPS):
            cols = slice(a * 128, (a + 1) * 128)
            out = whole[0:STEP, cols]
            for q in range(1, PER):
                out = jnp.where(lane_group == q, whole[q * STEP : (q + 1) * STEP, cols], out)
            outs.append(out)
        return jnp.concatenate(outs, axis=0)

    def forward_conv(half):
        r0 = half * HALF

        def tile(c, carry):
            lanes = pl.ds(pl.multiple_of(c * 128, 128), 128)
            out = long_conv(toep_a, gated, r0, c, lanes)
            long_out[pl.ds(r0, HALF), lanes] = out
            mixer[pl.ds(r0, HALF), lanes] = (
                post[0, pl.ds(r0, HALF), lanes].astype(F32) * out
            ).astype(BF16)
            return carry

        lax.fori_loop(0, TILES, tile, 0, unroll=True)

    def project(half, side, place, owner):
        cols = pl.ds(pl.multiple_of(owner * OUT, OUT), OUT)
        part = dot(mixer[pl.ds(half * HALF, HALF), :], w[:, cols]).astype(BF16)
        psum_q[half, side, place, 0 : QR[half]] = part[0 : QR[half]]
        psum_p[half, place, side, 0 : PR[half]] = part[QR[half] : HALF]

    def rs_copy(n, half, src, dst, dev):
        return remote(src, dst, rs_s.at[half, n], rs_r.at[half, n], (ctx, dev))

    def rs_all(half):
        p = pl.ds(0, PR[half])
        q = pl.ds(0, QR[half])

        def raw_q(n, place):
            return rs_copy(n, half, psum_q.at[half, 1, place, q], in_q.at[half, place, q], xo)

        copies = [
            rs_copy(0, half, psum_p.at[half, 3, :, p], in_up.at[half, :, p], up),
            rs_copy(1, half, psum_p.at[half, 2, :, p], in_own_up.at[half, :, p], dn),
            raw_q(2, 3),
            raw_q(3, 2),
            raw_q(4, 1),
            raw_q(5, 0),
            rs_copy(6, half, psum_p.at[half, 1, :, p], in_own_dn.at[half, :, p], up),
            rs_copy(7, half, psum_q.at[half, 0, 3, q], in_q_up.at[half, q], up),
            rs_copy(8, half, psum_q.at[half, 0, 2, q], in_q_own_up.at[half, q], dn),
            rs_copy(9, half, psum_q.at[half, 0, 1, q], in_q_own_dn.at[half, q], up),
            rs_copy(10, half, psum_p.at[half, 0, 1, p], in_x.at[half, p], xo),
        ]
        return copies

    rs = [rs_all(0), rs_all(1)]

    def rs_start(half, n):
        rs[half][n].start()
        started.append(rs[half][n])

    def project_far(half):
        project(half, 1, 3, xop)
        project(half, 0, 3, op)
        rs_start(half, 2)
        rs_start(half, 0)

    def project_dn(half):
        project(half, 1, 2, xdn)
        project(half, 0, 2, dn)
        rs_start(half, 3)
        rs_start(half, 1)

    def project_up(half):
        project(half, 1, 1, xup)
        project(half, 1, 0, xo)
        rs_start(half, 4)
        rs_start(half, 5)
        project(half, 0, 1, up)
        project(half, 0, 0, me)

    def add(a, *others):
        total = a.astype(F32)
        for other in others:
            total = total + other.astype(F32)
        return total.astype(BF16)

    def q_rows(ref, half, *place):
        return ref[(half, *place, pl.ds(0, QR[half]))]

    def p_rows(ref, half, *place):
        return ref[(half, *place, pl.ds(0, PR[half]))]

    def rs_a(half):
        rs[half][2].wait_recv()
        psum_q[half, 0, 3, 0 : QR[half]] = add(q_rows(psum_q, half, 0, 3), q_rows(in_q, half, 3))
        rs_start(half, 7)

    def rs_b(half):
        rs[half][0].wait_recv()
        for side in (0, 1):
            psum_p[half, 1, side, 0 : PR[half]] = add(
                p_rows(psum_p, half, 1, side), p_rows(in_up, half, side)
            )
        rs_start(half, 6)

    def rs_c(half):
        rs[half][3].wait_recv()
        psum_q[half, 0, 2, 0 : QR[half]] = add(q_rows(psum_q, half, 0, 2), q_rows(in_q, half, 2))
        rs_start(half, 8)

    def rs_d(half):
        rs[half][4].wait_recv()
        rs[half][7].wait_recv()
        psum_q[half, 0, 1, 0 : QR[half]] = add(
            q_rows(psum_q, half, 0, 1), q_rows(in_q, half, 1), q_rows(in_q_up, half)
        )
        rs_start(half, 9)

    def rs_e(half):
        rs[half][1].wait_recv()
        rs[half][6].wait_recv()
        psum_p[half, 0, 1, 0 : PR[half]] = add(
            p_rows(psum_p, half, 0, 1), p_rows(in_own_dn, half, 1), p_rows(in_own_up, half, 1)
        )
        rs_start(half, 10)

    def rs_last(half):
        rs[half][5].wait_recv()
        rs[half][8].wait_recv()
        rs[half][9].wait_recv()
        out_mixed[part_rows(half, QS), :] = add(
            q_rows(psum_q, half, 0, 0),
            q_rows(in_q, half, 0),
            q_rows(in_q_own_dn, half),
            q_rows(in_q_own_up, half),
        )
        rs[half][10].wait_recv()
        out_mixed[part_rows(half, PS), :] = add(
            p_rows(psum_p, half, 0, 0),
            p_rows(in_own_dn, half, 0),
            p_rows(in_own_up, half, 0),
            p_rows(in_x, half),
        )

    def d_mixer(slots, start, last):
        for c in range(CHAN // 256):
            chans = pl.ds(c * 256, 256)
            total = None if start else d_acc[chans, :]
            for s in slots:
                cols = pl.ds(pl.multiple_of(s * OUT, OUT), OUT)
                part = dot(w[chans, cols], gath[s], ((1,), (1,)))
                total = part if total is None else total + part
            if not last:
                d_acc[chans, :] = total
                continue
            grad = total.T.astype(BF16).astype(F32)
            d_post[0, pl.ds(0, ROWS), chans] = grad * long_out[:, chans]
            d_long[pl.ds(0, ROWS), chans] = (grad * post[0, :, chans].astype(F32)).astype(BF16)

    def ag_wait_both(*which):
        for half in (0, 1):
            for n, slot, part in which:
                ag_wait(n, half, slot, part)

    wide_group = lax.rem(lax.broadcasted_iota(jnp.int32, (STEP, 2 * CHAN), 1), 128) // 16

    def correlate():
        for c in range(TILES):
            lanes = pl.ds(c * 128, 128)
            grads = jnp.concatenate(
                [d_long[pl.ds(STEP * a, STEP), lanes] for a in range(2 * STEPS)], axis=1
            )
            stack = jnp.concatenate(
                [jnp.where(wide_group == q, grads, jnp.zeros_like(grads)) for q in range(PER)],
                axis=0,
            )
            window = jnp.concatenate(
                [gated[pl.ds(STEP * a, SPAN), lanes] for a in range(2 * STEPS)], axis=1
            )
            whole = dot(stack, window, ((1,), (1,)))
            there = pl.ds(c * HALF, HALF)
            corr_lo[there, :] = whole[:, 0:128]
            corr_hi[there, 0:STEP] = whole[:, 128:SPAN]

    def corr_row(b):
        rows = pl.ds(b, GROUPS, stride=STEP)
        return jnp.concatenate([corr_lo[rows, :], corr_hi[rows, :]], axis=1)

    def filter_sums():
        taps_sum = corr_row(0)
        for b in range(1, STEP):
            taps_sum = taps_sum + pltpu.roll(corr_row(b), 2 * HALF - b, 1)
        lane_i = lax.broadcasted_iota(jnp.int32, (GROUPS, 2 * HALF), 1)
        taps_sum = jnp.where((lane_i >= 1) & (lane_i <= HALF), taps_sum, 0.0)
        fpart[...] = lax.dot_general(
            taps_sum,
            (cols_i == HALF - rows_i).astype(F32),
            (((1,), (1,)), ((), ())),
            preferred_element_type=F32,
            precision=lax.Precision.HIGHEST,
        ).reshape(QUAD, SHARE, HALF)

    def quad_copy(src, dst, k, base):
        return remote(src, dst, fg_s.at[base + k], fg_r.at[base + k], (quads[k - 1], me))

    def filter_first():
        for k in range(1, QUAD):
            copy = quad_copy(fpart.at[lax.rem(quad + k, QUAD)], fcore.at[quad], k, 0)
            copy.start()
            started.append(copy)

    def filter_second():
        own_sum = fpart[quad]
        for k in range(1, QUAD):
            slot = lax.rem(quad + QUAD - k, QUAD)
            here = fcore.at[slot]
            quad_copy(here, here, k, 0).wait_recv()
            own_sum = own_sum + fcore[slot]
        fsum[...] = own_sum

        @pl.when(ring < RINGS - 1)
        def _():
            pl.semaphore_wait(far, RINGS - 1 - ring)

        for k in range(1, RINGS):
            copy = remote(
                fsum, fall.at[ring], fg_s.at[3 + k], fg_r.at[3 + k], (along[k - 1], me)
            )
            copy.start()
            started.append(copy)

    def filter_third():
        total = fsum[...]
        for k in range(1, RINGS):
            slot = lax.rem(ring + RINGS - k, RINGS)
            here = fall.at[slot]
            remote(here, here, fg_s.at[3 + k], fg_r.at[3 + k], (along[k - 1], me)).wait_recv()
            total = total + fall[slot]
        fout[quad] = total * ((N_CTX * ROWS * 16) ** -0.5)
        for k in range(1, QUAD):
            here = fout.at[quad]
            copy = quad_copy(here, here, k, 10)
            copy.start()
            started.append(copy)

    def filter_last():
        for k in range(1, QUAD):
            here = fout.at[lax.rem(quad + QUAD - k, QUAD)]
            quad_copy(here, here, k, 10).wait_recv()
        filt[...] = fout[...].reshape(GROUPS, HALF)

    def backward_conv(half):
        r0 = half * HALF

        def tile(c, carry):
            lanes = pl.ds(pl.multiple_of(c * 128, 128), 128)
            out = long_conv(toep_b, d_long, r0, c, lanes)
            for i in (1, 2):
                d_post[i, pl.ds(r0, HALF), lanes] = out * post[
                    3 - i, pl.ds(r0, HALF), lanes
                ].astype(F32)
            return carry

        lax.fori_loop(0, TILES, tile, 0, unroll=True)

    def short_back(half):
        r0 = half * HALF

        def tile(c, carry):
            lanes = pl.ds(pl.multiple_of(c * 128, 128), 128)
            for i in range(3):
                ext = d_post[i, pl.ds(r0, HALF + 8), lanes]
                taps = sf[i, :, lanes].astype(F32)
                out_grads[i, pl.ds(r0, HALF), lanes] = (
                    taps[0:1] * ext[0:HALF]
                    + taps[1:2] * ext[1 : 1 + HALF]
                    + taps[2:3] * ext[2 : 2 + HALF]
                ).astype(BF16)
            return carry

        lax.fori_loop(0, TILES, tile, 0, unroll=True)

    def halo(n, src, dst, dev):
        return remote(src, dst, halo_s.at[n], halo_r.at[n], (dev, me))

    feat_halo = halo(0, feat.at[:, pl.ds(ROWS - 16, 16), :], feats.at[:, pl.ds(0, 16), :], nxt)
    gated_halo = halo(1, gated.at[pl.ds(2 * HALF, HALF), :], gated.at[pl.ds(0, HALF), :], nxt)
    long_halo = halo(2, d_long.at[pl.ds(0, HALF), :], d_long.at[pl.ds(2 * HALF, HALF), :], prv)
    post_halo = halo(3, d_post.at[:, pl.ds(0, 8), :], d_post.at[:, pl.ds(ROWS, 8), :], prv)

    def halo_start(copy, none):
        @pl.when(jnp.logical_not(none))
        def _():
            copy.start()

    def halo_wait(copy, none, ref, shape):
        @pl.when(none)
        def _():
            ref[...] = jnp.zeros(shape, ref.dtype)

        @pl.when(jnp.logical_not(none))
        def _():
            copy.wait_recv()

    halo_start(feat_halo, final)
    own_p(0)
    own_q(0)
    for k in range(1, RINGS):

        @pl.when(ring - k >= 0)
        def _(k=k):
            greet(far, (lax.rem(ctx + N_CTX - QUAD * k, N_CTX), me))

    own_q(1)
    own_p(1)
    own_r(1)
    pass_q_dn(1)
    own_r(0)
    build(vec_b, toep_b)
    pass_q_dn(0)
    load_f.wait()
    short_conv(1)
    halo_start(gated_halo, final)
    pass_p(0)
    pass_p(1)
    load_w.wait()
    load_c.wait()
    ag_wait_both((1, xo, QS))
    d_mixer((me, xo), True, False)
    pass_dn(0)
    pass_q_up(1)
    halo_wait(feat_halo, first, feats.at[:, pl.ds(0, 16), :], (3, 16, CHAN))
    short_conv(0)
    pass_dn(1)
    pass_q_up(0)
    ag_wait_both((5, up, PS))
    d_mixer((dn, up), False, False)
    pass_op(1)
    pass_xdn(0)
    pass_xdn(1)
    pass_op(0)
    forward_conv(1)
    project_far(1)
    project_dn(1)
    ag_wait_both((7, xup, PS), (9, xdn, QS), (10, xup, QS))
    d_mixer((xup, xdn), False, False)
    halo_wait(gated_halo, first, gated.at[pl.ds(0, HALF), :], (HALF, CHAN))
    forward_conv(0)
    project_far(0)
    ag_wait_both((11, op, PS))
    d_mixer((op,), False, False)
    project_dn(0)
    ag_wait_both((12, xop, QS), (13, xop, PS))
    d_mixer((xop,), False, True)
    halo_start(long_halo, first)
    correlate()
    filter_sums()
    filter_first()
    project_up(1)
    rs_b(1)
    project_up(0)
    rs_a(1)
    rs_b(0)
    filter_second()
    backward_conv(0)
    halo_start(post_halo, first)
    rs_a(0)
    rs_e(1)
    rs_c(0)
    rs_c(1)
    rs_d(1)
    halo_wait(long_halo, final, d_long.at[pl.ds(2 * HALF, HALF), :], (HALF, CHAN))
    backward_conv(1)
    rs_e(0)
    filter_third()
    rs_d(0)
    rs_last(1)
    halo_wait(post_halo, final, d_post.at[:, pl.ds(ROWS, 8), :], (3, 8, CHAN))
    short_back(0)
    short_back(1)
    store_g = pltpu.make_async_copy(out_grads, fgrads, lsem.at[3])
    store_g.start()
    rs_last(0)
    store_m = pltpu.make_async_copy(out_mixed, mixed, lsem.at[4])
    store_m.start()
    filter_last()

    for copy in started:
        copy.wait_send()

    @pl.when(jnp.logical_not(final))
    def _():
        feat_halo.wait_send()
        gated_halo.wait_send()

    @pl.when(jnp.logical_not(first))
    def _():
        long_halo.wait_send()
        post_halo.wait_send()

    store_g.wait()
    store_m.wait()


def publish(mixed, fgrads, filt, out_mixed, out_fgrads, out_filt, hold_m, hold_g, hold_f, sem):
    pairs = [(fgrads.at[i], hold_g.at[i], out_fgrads.at[i]) for i in range(3)]
    pairs += [(mixed, hold_m, out_mixed), (filt, hold_f, out_filt)]
    loads = [
        pltpu.make_async_copy(src, mid, sem.at[n]) for n, (src, mid, _) in enumerate(pairs)
    ]
    stores = [
        pltpu.make_async_copy(mid, dst, sem.at[5 + n]) for n, (_, mid, dst) in enumerate(pairs)
    ]
    for load in loads:
        load.start()
    for load, store in zip(loads, stores):
        load.wait()
        store.start()
    for store in stores:
        store.wait()


def on_device(features, short_filter, long_filter, out_weight, out_cotangent):
    hbm = pl.BlockSpec(memory_space=pl.ANY)
    vmem = pl.BlockSpec(memory_space=pltpu.VMEM)
    dma = pltpu.SemaphoreType.DMA
    scratch = [
        pltpu.VMEM((3, ROWS + 16, CHAN), BF16),
        pltpu.VMEM((3, ROWS, CHAN), BF16),
        pltpu.VMEM((ROWS + HALF, CHAN), BF16),
        pltpu.VMEM((ROWS, CHAN), F32),
        pltpu.VMEM((ROWS, CHAN), BF16),
        pltpu.VMEM((GROUPS * STEP, 2 * HALF), BF16),
        pltpu.VMEM((GROUPS * STEP, 2 * HALF), BF16),
        pltpu.VMEM((GROUPS, 2 * HALF), F32),
        pltpu.VMEM((GROUPS, 2 * HALF), F32),
        pltpu.VMEM((N_TP, ROWS, OUT), BF16),
        pltpu.VMEM((CHAN, N_TP * OUT), BF16),
        pltpu.VMEM((2, 4, 2, PM, OUT), BF16),
        pltpu.VMEM((2, 2, 4, QM, OUT), BF16),
        pltpu.VMEM((2, 2, PM, OUT), BF16),
        pltpu.VMEM((2, 2, PM, OUT), BF16),
        pltpu.VMEM((2, 2, PM, OUT), BF16),
        pltpu.VMEM((2, PM, OUT), BF16),
        pltpu.VMEM((2, 4, QM, OUT), BF16),
        pltpu.VMEM((2, QM, OUT), BF16),
        pltpu.VMEM((2, QM, OUT), BF16),
        pltpu.VMEM((2, QM, OUT), BF16),
        pltpu.VMEM((ROWS + HALF, CHAN), BF16),
        pltpu.VMEM((3, ROWS + 8, CHAN), F32),
        pltpu.VMEM((GROUPS * STEP, HALF), F32),
        pltpu.VMEM((GROUPS * STEP, HALF), F32),
        pltpu.VMEM((CHAN, ROWS), F32),
        pltpu.VMEM((QUAD, SHARE, HALF), F32),
        pltpu.VMEM((QUAD, SHARE, HALF), F32),
        pltpu.VMEM((SHARE, HALF), F32),
        pltpu.VMEM((RINGS, SHARE, HALF), F32),
        pltpu.VMEM((QUAD, SHARE, HALF), F32),
        pltpu.VMEM((ROWS, OUT), BF16),
        pltpu.VMEM((3, ROWS, CHAN), BF16),
        dma((5,)),
        dma((2, 14)),
        dma((2, 14)),
        dma((2, 11)),
        dma((2, 11)),
        dma((4,)),
        dma((4,)),
        dma((14,)),
        dma((14,)),
        pltpu.SemaphoreType.REGULAR,
    ]
    shapes = (
        jax.ShapeDtypeStruct((ROWS, OUT), BF16),
        jax.ShapeDtypeStruct((3, ROWS, CHAN), BF16),
        jax.ShapeDtypeStruct((GROUPS, HALF), F32),
    )
    results = pl.pallas_call(
        kernel,
        out_shape=shapes,
        in_specs=[hbm, vmem, vmem, hbm, hbm],
        out_specs=(hbm, hbm, vmem),
        scratch_shapes=scratch,
        compiler_params=pltpu.CompilerParams(
            collective_id=0, has_side_effects=True, vmem_limit_bytes=56 * 2**20
        ),
    )(features, short_filter, long_filter, out_weight, out_cotangent)
    return pl.pallas_call(
        publish,
        out_shape=shapes,
        in_specs=[hbm] * 3,
        out_specs=(hbm,) * 3,
        scratch_shapes=[
            pltpu.VMEM((ROWS, OUT), BF16),
            pltpu.VMEM((3, ROWS, CHAN), BF16),
            pltpu.VMEM((GROUPS, HALF), F32),
            dma((10,)),
        ],
    )(*results)


def solution(mesh):
    placed = (
        P(None, "ctx", "tp"),
        P(None, None, "tp"),
        P("tp", None),
        P("tp", None),
        P("ctx", "tp"),
    )
    return jax.shard_map(
        on_device,
        mesh=mesh,
        in_specs=placed,
        out_specs=(P("ctx", "tp"), P(None, "ctx", "tp"), P("tp", None)),
        check_vma=False,
    )
```

```python
import functools

import jax
import jax.numpy as jnp
from jax import lax
from jax.experimental import pallas as pl
from jax.experimental.pallas import tpu as pltpu
from jax.sharding import PartitionSpec as P

MESH = pl.DeviceIdType.MESH
F32 = jnp.float32
BF16 = jnp.bfloat16
ROWS = 256
HALF = 128
CHAN = 1024
OUT = 512
N_TP = 8
N_CTX = 32
GROUPS = 64
QR = (48, 32)
PR = (HALF - QR[0], HALF - QR[1])
QM = max(QR)
PM = max(PR)
TILES = CHAN // 128
PER = 8
QUAD = 4
RINGS = N_CTX // QUAD
SHARE = GROUPS // QUAD
STEP = 16
SPAN = HALF + STEP
STEPS = HALF // STEP


def dot(a, b, dims=((1,), (0,))):
    return lax.dot_general(a, b, (dims, ((), ())), preferred_element_type=F32)


def kernel(
    feat,
    sf,
    lf,
    w_hbm,
    cot,
    mixed,
    fgrads,
    filt,
    feats,
    post,
    gated,
    long_out,
    mixer,
    toep_a,
    toep_b,
    vec_a,
    vec_b,
    gath,
    w,
    psum_p,
    psum_q,
    in_up,
    in_own_dn,
    in_own_up,
    in_x,
    in_q,
    in_q_up,
    in_q_own_dn,
    in_q_own_up,
    d_long,
    d_post,
    corr_lo,
    corr_hi,
    d_acc,
    fpart,
    fcore,
    fsum,
    fall,
    fout,
    out_mixed,
    out_grads,
    lsem,
    ag_s,
    ag_r,
    rs_s,
    rs_r,
    halo_s,
    halo_r,
    fg_s,
    fg_r,
    far,
):
    ctx = lax.axis_index("ctx")
    me = lax.axis_index("tp")
    core = lax.rem(ctx, 2)
    quad = lax.rem(ctx, QUAD)
    ring = ctx // QUAD
    corner = ctx - quad
    xl = me // 4
    yl = lax.rem(me, 4)
    step = 1 + 2 * core
    back = 3 - 2 * core
    y_up = lax.rem(yl + step, 4)
    y_dn = lax.rem(yl + back, 4)
    y_op = lax.rem(yl + 2, 4)
    own_base = xl * 4
    x_base = 4 - xl * 4
    up = own_base + y_up
    dn = own_base + y_dn
    op = own_base + y_op
    xo = x_base + yl
    xup = x_base + y_up
    xdn = x_base + y_dn
    xop = x_base + y_op
    nxt = lax.rem(ctx + 1, N_CTX)
    prv = lax.rem(ctx + N_CTX - 1, N_CTX)

    load_f = pltpu.make_async_copy(feat, feats.at[:, pl.ds(16, ROWS), :], lsem.at[0])
    load_w = pltpu.make_async_copy(w_hbm, w, lsem.at[1])
    load_c = pltpu.make_async_copy(cot, gath.at[me], lsem.at[2])
    load_f.start()
    load_w.start()
    load_c.start()

    first = ctx == 0
    final = ctx == N_CTX - 1
    barrier = pltpu.get_barrier_semaphore()

    def greet(sem, dev):
        pl.semaphore_signal(sem, inc=1, device_id=dev, device_id_type=MESH)

    across = core * nxt + (1 - core) * prv
    quads = [corner + lax.rem(quad + k, QUAD) for k in range(1, QUAD)]
    along = [lax.rem(ring + k, RINGS) * QUAD + quad for k in range(1, RINGS)]
    for near in [(ctx, xo), (ctx, up), (ctx, dn)] + [(dev, me) for dev in quads]:
        greet(barrier, near)

    @pl.when(jnp.logical_not(first | final))
    def _():
        greet(barrier, (across, me))

    for k in range(1, RINGS):

        @pl.when(ring + k < RINGS)
        def _(k=k):
            greet(barrier, (along[k - 1], me))

    rows_i = lax.broadcasted_iota(jnp.int32, (HALF, 2 * HALF), 0)
    cols_i = lax.broadcasted_iota(jnp.int32, (HALF, 2 * HALF), 1)
    flip = (cols_i == HALF - rows_i).astype(BF16)
    keep = (cols_i == rows_i).astype(BF16)
    vec_a[...] = dot(lf[...], flip)
    vec_b[...] = dot(lf[...], keep)

    def build(vec, toep):
        def group(g, carry):
            row = jnp.broadcast_to(vec[pl.ds(g, 1), :], (STEP, 2 * HALF))
            there = pl.ds(pl.multiple_of(g * STEP, STEP), STEP)
            toep[there, :] = pltpu.roll(row, 0, 1, stride=1, stride_axis=0).astype(BF16)
            return carry

        lax.fori_loop(0, GROUPS, group, 0, unroll=8)

    build(vec_a, toep_a)
    ends = jnp.where(first | final, 0, 1)
    pl.semaphore_wait(barrier, 6 + ends + ring)

    started = []

    def remote(src, dst, send, recv, dev):
        return pltpu.make_async_remote_copy(
            src_ref=src,
            dst_ref=dst,
            send_sem=send,
            recv_sem=recv,
            device_id=dev,
            device_id_type=MESH,
        )

    QS, PS = 0, 1

    def part_rows(half, part):
        if part == QS:
            return pl.ds(half * HALF, QR[half])
        return pl.ds(half * HALF + QR[half], PR[half])

    def ag_view(slot, half, part):
        return gath.at[slot, part_rows(half, part), :]

    def ag_send(n, half, slot, part, dev, src=None):
        there = ag_view(slot, half, part)
        copy = remote(
            there if src is None else src,
            there,
            ag_s.at[half, n],
            ag_r.at[half, n],
            (ctx, dev),
        )
        copy.start()
        started.append(copy)

    def ag_wait(n, half, slot, part):
        there = ag_view(slot, half, part)
        remote(there, there, ag_s.at[half, n], ag_r.at[half, n], (ctx, xo)).wait_recv()

    def cot_view(half, part):
        return cot.at[part_rows(half, part), :]

    def own_p(half):
        ag_send(0, half, me, PS, xo, cot_view(half, PS))

    def own_q(half):
        ag_send(2, half, me, QS, up, cot_view(half, QS))
        ag_send(3, half, me, QS, dn, cot_view(half, QS))

    def own_r(half):
        ag_send(1, half, me, QS, xo, cot_view(half, QS))
        ag_send(4, half, me, PS, up, cot_view(half, PS))
        ag_send(5, half, me, PS, dn, cot_view(half, PS))

    def pass_q_dn(half):
        ag_wait(2, half, dn, QS)
        ag_send(8, half, dn, QS, up)
        ag_send(9, half, dn, QS, xo)

    def pass_q_up(half):
        ag_wait(3, half, up, QS)
        ag_send(10, half, up, QS, xo)

    def pass_p(half):
        ag_wait(0, half, xo, PS)
        ag_send(6, half, xo, PS, up)
        ag_send(7, half, xo, PS, dn)

    def pass_dn(half):
        ag_wait(4, half, dn, PS)
        ag_send(11, half, dn, PS, up)

    def pass_op(half):
        ag_wait(8, half, op, QS)
        ag_send(12, half, op, QS, xo)

    def pass_xdn(half):
        ag_wait(6, half, xdn, PS)
        ag_send(13, half, xdn, PS, up)

    def short_conv(half):
        r0 = half * HALF

        def tile(c, carry):
            lanes = pl.ds(pl.multiple_of(c * 128, 128), 128)
            kept = []
            for i in range(3):
                ext = feats[i, pl.ds(r0, HALF + 16), lanes].astype(F32)
                taps = sf[i, :, lanes].astype(F32)
                value = (
                    taps[0:1] * ext[16 : 16 + HALF]
                    + taps[1:2] * ext[15 : 15 + HALF]
                    + taps[2:3] * ext[14 : 14 + HALF]
                ).astype(BF16)
                post[i, pl.ds(r0, HALF), lanes] = value
                kept.append(value.astype(F32))
            gated[pl.ds(HALF + r0, HALF), lanes] = (kept[1] * kept[2]).astype(BF16)
            return carry

        lax.fori_loop(0, TILES, tile, 0, unroll=True)

    lane_group = lax.broadcasted_iota(jnp.int32, (STEP, 128), 1) // 16

    def long_conv(toep, source, r0, c, lanes):
        block = toep[pl.ds(pl.multiple_of(c * HALF, HALF), HALF), 0:SPAN]
        window = jnp.concatenate(
            [source[pl.ds(r0 + STEP * a, SPAN), lanes] for a in range(STEPS)], axis=1
        )
        whole = dot(block, window)
        outs = []
        for a in range(STEPS):
            cols = slice(a * 128, (a + 1) * 128)
            out = whole[0:STEP, cols]
            for q in range(1, PER):
                out = jnp.where(lane_group == q, whole[q * STEP : (q + 1) * STEP, cols], out)
            outs.append(out)
        return jnp.concatenate(outs, axis=0)

    def forward_conv(half):
        r0 = half * HALF

        def tile(c, carry):
            lanes = pl.ds(pl.multiple_of(c * 128, 128), 128)
            out = long_conv(toep_a, gated, r0, c, lanes)
            long_out[pl.ds(r0, HALF), lanes] = out
            mixer[pl.ds(r0, HALF), lanes] = (
                post[0, pl.ds(r0, HALF), lanes].astype(F32) * out
            ).astype(BF16)
            return carry

        lax.fori_loop(0, TILES, tile, 0, unroll=True)

    def project(half, side, place, owner):
        cols = pl.ds(pl.multiple_of(owner * OUT, OUT), OUT)
        part = dot(mixer[pl.ds(half * HALF, HALF), :], w[:, cols]).astype(BF16)
        psum_q[half, side, place, 0 : QR[half]] = part[0 : QR[half]]
        psum_p[half, place, side, 0 : PR[half]] = part[QR[half] : HALF]

    def rs_copy(n, half, src, dst, dev):
        return remote(src, dst, rs_s.at[half, n], rs_r.at[half, n], (ctx, dev))

    def rs_all(half):
        p = pl.ds(0, PR[half])
        q = pl.ds(0, QR[half])

        def raw_q(n, place):
            return rs_copy(n, half, psum_q.at[half, 1, place, q], in_q.at[half, place, q], xo)

        copies = [
            rs_copy(0, half, psum_p.at[half, 3, :, p], in_up.at[half, :, p], up),
            rs_copy(1, half, psum_p.at[half, 2, :, p], in_own_up.at[half, :, p], dn),
            raw_q(2, 3),
            raw_q(3, 2),
            raw_q(4, 1),
            raw_q(5, 0),
            rs_copy(6, half, psum_p.at[half, 1, :, p], in_own_dn.at[half, :, p], up),
            rs_copy(7, half, psum_q.at[half, 0, 3, q], in_q_up.at[half, q], up),
            rs_copy(8, half, psum_q.at[half, 0, 2, q], in_q_own_up.at[half, q], dn),
            rs_copy(9, half, psum_q.at[half, 0, 1, q], in_q_own_dn.at[half, q], up),
            rs_copy(10, half, psum_p.at[half, 0, 1, p], in_x.at[half, p], xo),
        ]
        return copies

    rs = [rs_all(0), rs_all(1)]

    def rs_start(half, n):
        rs[half][n].start()
        started.append(rs[half][n])

    def project_far(half):
        project(half, 1, 3, xop)
        project(half, 0, 3, op)
        rs_start(half, 2)
        rs_start(half, 0)

    def project_dn(half):
        project(half, 1, 2, xdn)
        project(half, 0, 2, dn)
        rs_start(half, 3)
        rs_start(half, 1)

    def project_up(half):
        project(half, 1, 1, xup)
        project(half, 1, 0, xo)
        rs_start(half, 4)
        rs_start(half, 5)
        project(half, 0, 1, up)
        project(half, 0, 0, me)

    def add(a, *others):
        total = a.astype(F32)
        for other in others:
            total = total + other.astype(F32)
        return total.astype(BF16)

    def q_rows(ref, half, *place):
        return ref[(half, *place, pl.ds(0, QR[half]))]

    def p_rows(ref, half, *place):
        return ref[(half, *place, pl.ds(0, PR[half]))]

    def rs_a(half):
        rs[half][2].wait_recv()
        psum_q[half, 0, 3, 0 : QR[half]] = add(q_rows(psum_q, half, 0, 3), q_rows(in_q, half, 3))
        rs_start(half, 7)

    def rs_b(half):
        rs[half][0].wait_recv()
        for side in (0, 1):
            psum_p[half, 1, side, 0 : PR[half]] = add(
                p_rows(psum_p, half, 1, side), p_rows(in_up, half, side)
            )
        rs_start(half, 6)

    def rs_c(half):
        rs[half][3].wait_recv()
        psum_q[half, 0, 2, 0 : QR[half]] = add(q_rows(psum_q, half, 0, 2), q_rows(in_q, half, 2))
        rs_start(half, 8)

    def rs_d(half):
        rs[half][4].wait_recv()
        rs[half][7].wait_recv()
        psum_q[half, 0, 1, 0 : QR[half]] = add(
            q_rows(psum_q, half, 0, 1), q_rows(in_q, half, 1), q_rows(in_q_up, half)
        )
        rs_start(half, 9)

    def rs_e(half):
        rs[half][1].wait_recv()
        rs[half][6].wait_recv()
        psum_p[half, 0, 1, 0 : PR[half]] = add(
            p_rows(psum_p, half, 0, 1), p_rows(in_own_dn, half, 1), p_rows(in_own_up, half, 1)
        )
        rs_start(half, 10)

    def rs_last(half):
        rs[half][5].wait_recv()
        rs[half][8].wait_recv()
        rs[half][9].wait_recv()
        out_mixed[part_rows(half, QS), :] = add(
            q_rows(psum_q, half, 0, 0),
            q_rows(in_q, half, 0),
            q_rows(in_q_own_dn, half),
            q_rows(in_q_own_up, half),
        )
        rs[half][10].wait_recv()
        out_mixed[part_rows(half, PS), :] = add(
            p_rows(psum_p, half, 0, 0),
            p_rows(in_own_dn, half, 0),
            p_rows(in_own_up, half, 0),
            p_rows(in_x, half),
        )

    def d_mixer(slots, start, last):
        for c in range(CHAN // 256):
            chans = pl.ds(c * 256, 256)
            total = None if start else d_acc[chans, :]
            for s in slots:
                cols = pl.ds(pl.multiple_of(s * OUT, OUT), OUT)
                part = dot(w[chans, cols], gath[s], ((1,), (1,)))
                total = part if total is None else total + part
            if not last:
                d_acc[chans, :] = total
                continue
            grad = total.T.astype(BF16).astype(F32)
            d_post[0, pl.ds(0, ROWS), chans] = grad * long_out[:, chans]
            d_long[pl.ds(0, ROWS), chans] = (grad * post[0, :, chans].astype(F32)).astype(BF16)

    def ag_wait_both(*which):
        for half in (0, 1):
            for n, slot, part in which:
                ag_wait(n, half, slot, part)

    wide_group = lax.rem(lax.broadcasted_iota(jnp.int32, (STEP, 2 * CHAN), 1), 128) // 16

    def correlate():
        for c in range(TILES):
            lanes = pl.ds(c * 128, 128)
            grads = jnp.concatenate(
                [d_long[pl.ds(STEP * a, STEP), lanes] for a in range(2 * STEPS)], axis=1
            )
            stack = jnp.concatenate(
                [jnp.where(wide_group == q, grads, jnp.zeros_like(grads)) for q in range(PER)],
                axis=0,
            )
            window = jnp.concatenate(
                [gated[pl.ds(STEP * a, SPAN), lanes] for a in range(2 * STEPS)], axis=1
            )
            whole = dot(stack, window, ((1,), (1,)))
            there = pl.ds(c * HALF, HALF)
            corr_lo[there, :] = whole[:, 0:128]
            corr_hi[there, 0:STEP] = whole[:, 128:SPAN]

    def corr_row(b):
        rows = pl.ds(b, GROUPS, stride=STEP)
        return jnp.concatenate([corr_lo[rows, :], corr_hi[rows, :]], axis=1)

    def filter_sums():
        taps_sum = corr_row(0)
        for b in range(1, STEP):
            taps_sum = taps_sum + pltpu.roll(corr_row(b), 2 * HALF - b, 1)
        lane_i = lax.broadcasted_iota(jnp.int32, (GROUPS, 2 * HALF), 1)
        taps_sum = jnp.where((lane_i >= 1) & (lane_i <= HALF), taps_sum, 0.0)
        fpart[...] = lax.dot_general(
            taps_sum,
            (cols_i == HALF - rows_i).astype(F32),
            (((1,), (1,)), ((), ())),
            preferred_element_type=F32,
            precision=lax.Precision.HIGHEST,
        ).reshape(QUAD, SHARE, HALF)

    def quad_copy(src, dst, k, base):
        return remote(src, dst, fg_s.at[base + k], fg_r.at[base + k], (quads[k - 1], me))

    def filter_first():
        for k in range(1, QUAD):
            copy = quad_copy(fpart.at[lax.rem(quad + k, QUAD)], fcore.at[quad], k, 0)
            copy.start()
            started.append(copy)

    def filter_second():
        own_sum = fpart[quad]
        for k in range(1, QUAD):
            slot = lax.rem(quad + QUAD - k, QUAD)
            here = fcore.at[slot]
            quad_copy(here, here, k, 0).wait_recv()
            own_sum = own_sum + fcore[slot]
        fsum[...] = own_sum

        @pl.when(ring < RINGS - 1)
        def _():
            pl.semaphore_wait(far, RINGS - 1 - ring)

        for k in range(1, RINGS):
            copy = remote(
                fsum, fall.at[ring], fg_s.at[3 + k], fg_r.at[3 + k], (along[k - 1], me)
            )
            copy.start()
            started.append(copy)

    def filter_third():
        total = fsum[...]
        for k in range(1, RINGS):
            slot = lax.rem(ring + RINGS - k, RINGS)
            here = fall.at[slot]
            remote(here, here, fg_s.at[3 + k], fg_r.at[3 + k], (along[k - 1], me)).wait_recv()
            total = total + fall[slot]
        fout[quad] = total * ((N_CTX * ROWS * 16) ** -0.5)
        for k in range(1, QUAD):
            here = fout.at[quad]
            copy = quad_copy(here, here, k, 10)
            copy.start()
            started.append(copy)

    def filter_last():
        for k in range(1, QUAD):
            here = fout.at[lax.rem(quad + QUAD - k, QUAD)]
            quad_copy(here, here, k, 10).wait_recv()
        filt[...] = fout[...].reshape(GROUPS, HALF)

    def backward_conv(half):
        r0 = half * HALF

        def tile(c, carry):
            lanes = pl.ds(pl.multiple_of(c * 128, 128), 128)
            out = long_conv(toep_b, d_long, r0, c, lanes)
            for i in (1, 2):
                d_post[i, pl.ds(r0, HALF), lanes] = out * post[
                    3 - i, pl.ds(r0, HALF), lanes
                ].astype(F32)
            return carry

        lax.fori_loop(0, TILES, tile, 0, unroll=True)

    def short_back(half):
        r0 = half * HALF

        def tile(c, carry):
            lanes = pl.ds(pl.multiple_of(c * 128, 128), 128)
            for i in range(3):
                ext = d_post[i, pl.ds(r0, HALF + 8), lanes]
                taps = sf[i, :, lanes].astype(F32)
                out_grads[i, pl.ds(r0, HALF), lanes] = (
                    taps[0:1] * ext[0:HALF]
                    + taps[1:2] * ext[1 : 1 + HALF]
                    + taps[2:3] * ext[2 : 2 + HALF]
                ).astype(BF16)
            return carry

        lax.fori_loop(0, TILES, tile, 0, unroll=True)

    def halo(n, src, dst, dev):
        return remote(src, dst, halo_s.at[n], halo_r.at[n], (dev, me))

    feat_halo = halo(0, feat.at[:, pl.ds(ROWS - 16, 16), :], feats.at[:, pl.ds(0, 16), :], nxt)
    gated_halo = halo(1, gated.at[pl.ds(2 * HALF, HALF), :], gated.at[pl.ds(0, HALF), :], nxt)
    long_halo = halo(2, d_long.at[pl.ds(0, HALF), :], d_long.at[pl.ds(2 * HALF, HALF), :], prv)
    post_halo = halo(3, d_post.at[:, pl.ds(0, 8), :], d_post.at[:, pl.ds(ROWS, 8), :], prv)

    def halo_start(copy, none):
        @pl.when(jnp.logical_not(none))
        def _():
            copy.start()

    def halo_wait(copy, none, ref, shape):
        @pl.when(none)
        def _():
            ref[...] = jnp.zeros(shape, ref.dtype)

        @pl.when(jnp.logical_not(none))
        def _():
            copy.wait_recv()

    halo_start(feat_halo, final)
    own_p(0)
    own_q(0)
    for k in range(1, RINGS):

        @pl.when(ring - k >= 0)
        def _(k=k):
            greet(far, (lax.rem(ctx + N_CTX - QUAD * k, N_CTX), me))

    own_q(1)
    own_p(1)
    own_r(1)
    pass_q_dn(1)
    own_r(0)
    build(vec_b, toep_b)
    pass_q_dn(0)
    load_f.wait()
    short_conv(1)
    halo_start(gated_halo, final)
    pass_p(0)
    pass_p(1)
    load_w.wait()
    load_c.wait()
    ag_wait_both((1, xo, QS))
    d_mixer((me, xo), True, False)
    pass_dn(0)
    pass_q_up(1)
    halo_wait(feat_halo, first, feats.at[:, pl.ds(0, 16), :], (3, 16, CHAN))
    short_conv(0)
    pass_dn(1)
    pass_q_up(0)
    ag_wait_both((5, up, PS))
    d_mixer((dn, up), False, False)
    pass_op(1)
    pass_xdn(0)
    pass_xdn(1)
    pass_op(0)
    forward_conv(1)
    project_far(1)
    project_dn(1)
    ag_wait_both((7, xup, PS), (9, xdn, QS), (10, xup, QS))
    d_mixer((xup, xdn), False, False)
    halo_wait(gated_halo, first, gated.at[pl.ds(0, HALF), :], (HALF, CHAN))
    forward_conv(0)
    project_far(0)
    ag_wait_both((11, op, PS))
    d_mixer((op,), False, False)
    project_dn(0)
    ag_wait_both((12, xop, QS), (13, xop, PS))
    d_mixer((xop,), False, True)
    halo_start(long_halo, first)
    correlate()
    filter_sums()
    filter_first()
    project_up(1)
    project_up(0)
    rs_b(1)
    backward_conv(0)
    halo_start(post_halo, first)
    filter_second()
    rs_a(1)
    rs_b(0)
    rs_a(0)
    rs_e(1)
    rs_c(1)
    rs_c(0)
    rs_d(1)
    filter_third()
    halo_wait(long_halo, final, d_long.at[pl.ds(2 * HALF, HALF), :], (HALF, CHAN))
    backward_conv(1)
    rs_e(0)
    rs_d(0)
    rs_last(1)
    halo_wait(post_halo, final, d_post.at[:, pl.ds(ROWS, 8), :], (3, 8, CHAN))
    short_back(0)
    short_back(1)
    store_g = pltpu.make_async_copy(out_grads, fgrads, lsem.at[3])
    store_g.start()
    rs_last(0)
    store_m = pltpu.make_async_copy(out_mixed, mixed, lsem.at[4])
    store_m.start()
    filter_last()

    for copy in started:
        copy.wait_send()

    @pl.when(jnp.logical_not(final))
    def _():
        feat_halo.wait_send()
        gated_halo.wait_send()

    @pl.when(jnp.logical_not(first))
    def _():
        long_halo.wait_send()
        post_halo.wait_send()

    store_g.wait()
    store_m.wait()


def publish(mixed, fgrads, filt, out_mixed, out_fgrads, out_filt, hold_m, hold_g, hold_f, sem):
    pairs = [(fgrads.at[i], hold_g.at[i], out_fgrads.at[i]) for i in range(3)]
    pairs += [(mixed, hold_m, out_mixed), (filt, hold_f, out_filt)]
    loads = [
        pltpu.make_async_copy(src, mid, sem.at[n]) for n, (src, mid, _) in enumerate(pairs)
    ]
    stores = [
        pltpu.make_async_copy(mid, dst, sem.at[5 + n]) for n, (_, mid, dst) in enumerate(pairs)
    ]
    for load in loads:
        load.start()
    for load, store in zip(loads, stores):
        load.wait()
        store.start()
    for store in stores:
        store.wait()


def on_device(features, short_filter, long_filter, out_weight, out_cotangent):
    hbm = pl.BlockSpec(memory_space=pl.ANY)
    vmem = pl.BlockSpec(memory_space=pltpu.VMEM)
    dma = pltpu.SemaphoreType.DMA
    scratch = [
        pltpu.VMEM((3, ROWS + 16, CHAN), BF16),
        pltpu.VMEM((3, ROWS, CHAN), BF16),
        pltpu.VMEM((ROWS + HALF, CHAN), BF16),
        pltpu.VMEM((ROWS, CHAN), F32),
        pltpu.VMEM((ROWS, CHAN), BF16),
        pltpu.VMEM((GROUPS * STEP, 2 * HALF), BF16),
        pltpu.VMEM((GROUPS * STEP, 2 * HALF), BF16),
        pltpu.VMEM((GROUPS, 2 * HALF), F32),
        pltpu.VMEM((GROUPS, 2 * HALF), F32),
        pltpu.VMEM((N_TP, ROWS, OUT), BF16),
        pltpu.VMEM((CHAN, N_TP * OUT), BF16),
        pltpu.VMEM((2, 4, 2, PM, OUT), BF16),
        pltpu.VMEM((2, 2, 4, QM, OUT), BF16),
        pltpu.VMEM((2, 2, PM, OUT), BF16),
        pltpu.VMEM((2, 2, PM, OUT), BF16),
        pltpu.VMEM((2, 2, PM, OUT), BF16),
        pltpu.VMEM((2, PM, OUT), BF16),
        pltpu.VMEM((2, 4, QM, OUT), BF16),
        pltpu.VMEM((2, QM, OUT), BF16),
        pltpu.VMEM((2, QM, OUT), BF16),
        pltpu.VMEM((2, QM, OUT), BF16),
        pltpu.VMEM((ROWS + HALF, CHAN), BF16),
        pltpu.VMEM((3, ROWS + 8, CHAN), F32),
        pltpu.VMEM((GROUPS * STEP, HALF), F32),
        pltpu.VMEM((GROUPS * STEP, HALF), F32),
        pltpu.VMEM((CHAN, ROWS), F32),
        pltpu.VMEM((QUAD, SHARE, HALF), F32),
        pltpu.VMEM((QUAD, SHARE, HALF), F32),
        pltpu.VMEM((SHARE, HALF), F32),
        pltpu.VMEM((RINGS, SHARE, HALF), F32),
        pltpu.VMEM((QUAD, SHARE, HALF), F32),
        pltpu.VMEM((ROWS, OUT), BF16),
        pltpu.VMEM((3, ROWS, CHAN), BF16),
        dma((5,)),
        dma((2, 14)),
        dma((2, 14)),
        dma((2, 11)),
        dma((2, 11)),
        dma((4,)),
        dma((4,)),
        dma((14,)),
        dma((14,)),
        pltpu.SemaphoreType.REGULAR,
    ]
    shapes = (
        jax.ShapeDtypeStruct((ROWS, OUT), BF16),
        jax.ShapeDtypeStruct((3, ROWS, CHAN), BF16),
        jax.ShapeDtypeStruct((GROUPS, HALF), F32),
    )
    results = pl.pallas_call(
        kernel,
        out_shape=shapes,
        in_specs=[hbm, vmem, vmem, hbm, hbm],
        out_specs=(hbm, hbm, vmem),
        scratch_shapes=scratch,
        compiler_params=pltpu.CompilerParams(
            collective_id=0, has_side_effects=True, vmem_limit_bytes=56 * 2**20
        ),
    )(features, short_filter, long_filter, out_weight, out_cotangent)
    return pl.pallas_call(
        publish,
        out_shape=shapes,
        in_specs=[hbm] * 3,
        out_specs=(hbm,) * 3,
        scratch_shapes=[
            pltpu.VMEM((ROWS, OUT), BF16),
            pltpu.VMEM((3, ROWS, CHAN), BF16),
            pltpu.VMEM((GROUPS, HALF), F32),
            dma((10,)),
        ],
    )(*results)


def solution(mesh):
    placed = (
        P(None, "ctx", "tp"),
        P(None, None, "tp"),
        P("tp", None),
        P("tp", None),
        P("ctx", "tp"),
    )
    return jax.shard_map(
        on_device,
        mesh=mesh,
        in_specs=placed,
        out_specs=(P("ctx", "tp"), P(None, "ctx", "tp"), P("tp", None)),
        check_vma=False,
    )
```
